32 devices in a mesh: dp: 8 (over z, x), head: 4 (over y, core).
Axes of the slice: x: 2, y: 2, z: 4, core: 2. Of those that a mesh axis runs over, the one named last changes fastest.
Arguments:
- key_grads: bfloat16 [2, 4096, 2048], P(None, 'dp', 'head'), may hold values from -6 to 6
- value_grads: bfloat16 [2, 4096, 2048], P(None, 'dp', 'head'), may hold values from -6 to 6
- key_weight: bfloat16 [2, 3584, 2048], P(None, 'dp', 'head'), may hold values from -0.125 to 0.125
- value_weight: bfloat16 [2, 3584, 2048], P(None, 'dp', 'head'), may hold values from -0.125 to 0.125
- block_source: int32 [64], replicated, may hold values from 0 to 63, as said below
- hidden_mid: bfloat16 [4096, 3584], P('dp', 'head')
- mlp_out: bfloat16 [4096, 3584], P('dp', 'head')
- post_gain: bfloat16 [3584], P('head'), may hold values from 0.5 to 2
- final_gain: bfloat16 [3584], P('head'), may hold values from 0.5 to 2
- gate_pre: bfloat16 [4096, 7168], P('dp', 'head'), may hold values from -6 to 6
- up_pre: bfloat16 [4096, 7168], P('dp', 'head'), may hold values from -6 to 6
- down_weight: bfloat16 [7168, 3584], P('head', 'dp'), may hold values from -0.09375 to 0.09375
Outputs:
- resid_grad: bfloat16 [4096, 3584], P('dp', 'head')
- gate_grad: bfloat16 [4096, 7168], P('dp', 'head')
- up_grad: bfloat16 [4096, 7168], P('dp', 'head')
The draws below stay inside these ranges and needn't reach their ends.
Inputs may be any that keep to these rules, and one draw needn't show every extreme that they name: block_source is a permutation of the 64 row blocks. The decoder blocks of one device are blocks 8 * a to 8 * a + 7, and the encoder blocks of device b are blocks 8 * b to 8 * b + 7; at most 2 decoder blocks of one device fill encoder blocks of one device, and exactly 2 do for some pairs of devices in every draw.
All inputs are finite; a program needn't handle non-finite values.
Results may differ from the reference program's by a relative error of at most 0.02.
Values may be sent and summed in bfloat16 or wider, within the bound.
A program may use at most 64 MiB of HBM per device.

```python
import math
import jax
import jax.numpy as jnp
from jax import lax

D = 3584
KVH = 8
HD = 256
FFW = 7168
XL = 2
CAP = 2
TOKENS = 4096
BLK = 64
NBLK = 64
N_DP = 8
N_HEAD = 4


def field_scales(scale_key):
    row_key, col_key = jax.random.split(scale_key)
    row_scale = jnp.exp(jax.random.uniform(row_key, (TOKENS, 1), jnp.float32) * math.log(10.0))
    col_ramp = jnp.arange(D, dtype=jnp.float32)[None, :] / D * math.log(3.0)
    col_scale = jnp.exp(jax.random.uniform(col_key, (1, D), jnp.float32) * math.log(10.0) + col_ramp)
    return row_scale * col_scale


def draw_hidden_mid(key, part):
    key = jax.random.fold_in(key, 11)
    scale_key, value_key = jax.random.split(key, 2)
    scales = field_scales(scale_key) * 0.25
    values = jax.random.normal(value_key, (TOKENS, D), jnp.float32)
    return (values * scales).astype(jnp.bfloat16)


def draw_mlp_out(key, part):
    key = jax.random.fold_in(key, 23)
    scale_key, value_key = jax.random.split(key, 2)
    scales = field_scales(scale_key) * 0.25
    values = jax.random.normal(value_key, (TOKENS, D), jnp.float32)
    return (values * scales).astype(jnp.bfloat16)


def draw_block_source(key, part):
    key = jax.random.fold_in(key, 5)
    device_key, shift_key, slot_key, order_key = jax.random.split(key, 4)
    device_perm = jax.random.permutation(device_key, N_DP)
    device_shift = jax.random.permutation(shift_key, N_DP)
    slot_keys = jax.random.split(slot_key, N_DP)
    slot_perm = jax.vmap(lambda one_key: jax.random.permutation(one_key, N_DP))(slot_keys)
    group_of = slot_perm // CAP
    dest_device = device_perm[(device_shift[:, None] + group_of) % N_DP]
    flat_dest = dest_device.reshape(-1).astype(jnp.int32)
    priority = jax.random.permutation(order_key, NBLK)
    earlier = (flat_dest[:, None] == flat_dest[None, :]) & (priority[None, :] < priority[:, None])
    dest_slot = jnp.sum(earlier.astype(jnp.int32), axis=1).astype(jnp.int32)
    dest_block = flat_dest * N_DP + dest_slot
    return jnp.argsort(dest_block).astype(jnp.int32)


def block_levels(rng, extent, shards, smallest, top_value):
    def one(axis_at, shards_of):
        heights = jax.random.uniform(jax.random.fold_in(jax.random.fold_in(rng, 6), axis_at), (shards_of,), jnp.float32, smallest / len(shards), top_value / len(shards))
        return jnp.repeat(jnp.exp(heights), extent[axis_at] // shards_of).reshape((-1,) + (1,) * (len(extent) - axis_at - 1))

    factor_of = one(*shards[0])
    for cut in shards[1:]:
        factor_of = factor_of * one(*cut)
    return factor_of


def gaussian(own_key, shape, width, most, cuts=(), kind=jnp.bfloat16):
    level = block_levels(own_key, shape, cuts, -0.22, 0.18) if cuts else 1.0
    array = jax.random.normal(own_key, shape, jnp.float32) * width * level
    return jnp.minimum(jnp.maximum(array, -most), most).astype(kind)


def setup_inputs(seed: int = 0) -> dict:
    streams_of = jax.random.split(jax.random.key(seed), 13)
    key_grads = gaussian(streams_of[0], (XL, TOKENS, KVH * HD), 1.0, 6.0, ((1, 8), (2, 4)))
    value_grads = gaussian(streams_of[1], (XL, TOKENS, KVH * HD), 1.0, 6.0, ((1, 8), (2, 4)))
    key_weight = gaussian(streams_of[2], (XL, D, KVH * HD), (KVH * HD) ** -0.5, 0.125, ((1, 8), (2, 4)))
    value_weight = gaussian(streams_of[3], (XL, D, KVH * HD), (KVH * HD) ** -0.5, 0.125, ((1, 8), (2, 4)))
    block_source = draw_block_source(jax.random.fold_in(streams_of[12], 71), 0)
    hidden_mid = draw_hidden_mid(jax.random.fold_in(streams_of[12], 71), 0)
    mlp_out = draw_mlp_out(jax.random.fold_in(streams_of[12], 71), 0)
    post_gain = jnp.clip(jnp.exp(math.log(2.0) - 1.3862944 * jax.random.uniform(streams_of[7], (D,), jnp.float32) ** block_levels(streams_of[7], (D,), ((0, 4),), -0.2, 0.2)), 0.5, 2.0).astype(jnp.bfloat16)
    final_gain = jnp.clip(jnp.exp(math.log(2.0) - 1.3862944 * jax.random.uniform(streams_of[8], (D,), jnp.float32) ** block_levels(streams_of[8], (D,), ((0, 4),), -0.2, 0.2)), 0.5, 2.0).astype(jnp.bfloat16)
    gate_pre = gaussian(streams_of[9], (TOKENS, FFW), 1.5, 6.0, ((0, 8), (1, 4)))
    up_pre = gaussian(streams_of[10], (TOKENS, FFW), 1.5, 6.0, ((0, 8), (1, 4)))
    down_weight = gaussian(streams_of[11], (FFW, D), D ** -0.5, 0.09375, ((0, 4), (1, 8)))
    return {"key_grads": key_grads, "value_grads": value_grads, "key_weight": key_weight, "value_weight": value_weight, "block_source": block_source, "hidden_mid": hidden_mid, "mlp_out": mlp_out, "post_gain": post_gain, "final_gain": final_gain, "gate_pre": gate_pre, "up_pre": up_pre, "down_weight": down_weight}


epsilon = 1e-06

def gelu_parts(gate_value):
    activated, pullback = jax.vjp(lambda pre_act: jax.nn.gelu(pre_act, approximate=True), gate_value)
    return (activated, pullback(jnp.ones_like(gate_value))[0])

def reference(key_grads, value_grads, key_weight, value_weight, block_source, hidden_mid, mlp_out, post_gain, final_gain, gate_pre, up_pre, down_weight):
    group_cols = KVH * HD // N_HEAD
    memory_sum = jnp.zeros((TOKENS, D), jnp.float32)
    for group in range(N_HEAD):
        low = group * group_cols
        high = low + group_cols
        group_sum = jnp.zeros((TOKENS, D), jnp.float32)
        for layer in range(XL):
            group_sum = group_sum + jnp.dot(key_grads[layer][:, low:high], key_weight[layer][:, low:high].T, preferred_element_type=jnp.float32)
            group_sum = group_sum + jnp.dot(value_grads[layer][:, low:high], value_weight[layer][:, low:high].T, preferred_element_type=jnp.float32)
        memory_sum = memory_sum + group_sum.astype(jnp.bfloat16).astype(jnp.float32)
    dec_memory = memory_sum.astype(jnp.bfloat16)
    memory_grad = dec_memory.reshape(NBLK, BLK, D)[block_source.astype(jnp.int32)].reshape(TOKENS, D)
    mid_value = hidden_mid.astype(jnp.float32)
    out_value = mlp_out.astype(jnp.float32)
    gain_post = post_gain.astype(jnp.float32)
    gain_final = final_gain.astype(jnp.float32)
    out_scale = lax.rsqrt(lax.optimization_barrier(jnp.mean(out_value * out_value, axis=1, keepdims=True)) + epsilon)
    resid = mid_value + out_value * out_scale * gain_post
    resid_scale = lax.rsqrt(lax.optimization_barrier(jnp.mean(resid * resid, axis=1, keepdims=True)) + epsilon)
    norm_grad = memory_grad.astype(jnp.float32) * gain_final
    final_mean = resid_scale * lax.optimization_barrier(jnp.mean(norm_grad * resid, axis=1, keepdims=True))
    resid_total = resid_scale * (norm_grad - resid * resid_scale * final_mean)
    post_input = resid_total * gain_post
    post_mean = out_scale * lax.optimization_barrier(jnp.mean(post_input * out_value, axis=1, keepdims=True))
    post_grad = (out_scale * (post_input - out_value * out_scale * post_mean)).astype(jnp.bfloat16)
    hidden_grad = jnp.dot(post_grad, down_weight.T, preferred_element_type=jnp.float32)
    activated, slope = gelu_parts(gate_pre.astype(jnp.float32))
    gate_grad = (hidden_grad * up_pre.astype(jnp.float32) * slope).astype(jnp.bfloat16)
    up_grad = (hidden_grad * activated).astype(jnp.bfloat16)
    return (resid_total.astype(jnp.bfloat16), gate_grad, up_grad)
```

```python
import functools

import jax
import jax.numpy as jnp
from jax import lax
from jax.experimental import pallas as pl
from jax.experimental.pallas import tpu as pltpu
from jax.sharding import PartitionSpec as P

CAP = 2


epsilon = 1e-06


def gelu_parts(gate_value):
    activated, pullback = jax.vjp(
        lambda pre_act: jax.nn.gelu(pre_act, approximate=True), gate_value
    )
    return (activated, pullback(jnp.ones_like(gate_value))[0])


def repack(dec_memory, block_source, dev_blocks):
    row_count, col_share = dec_memory.shape
    block_rows = row_count // dev_blocks
    total_blocks = dev_blocks * dev_blocks
    slot_count = dev_blocks * CAP
    this_dev = lax.axis_index("dp")
    block_ids = jnp.arange(total_blocks, dtype=jnp.int32)
    is_source = block_source[:, None] == block_ids[None, :]
    dest_block = jnp.sum(jnp.where(is_source, block_ids[:, None], 0), axis=0)
    dest_device = (dest_block // dev_blocks).reshape(dev_blocks, dev_blocks)
    same_dest = dest_device[:, :, None] == dest_device[:, None, :]
    slot_ids = jnp.arange(dev_blocks, dtype=jnp.int32)
    before_slot = slot_ids[None, :] < slot_ids[:, None]
    dest_rank = jnp.sum((same_dest & before_slot[None, :, :]).astype(jnp.int32), axis=2)
    own_dest = lax.dynamic_index_in_dim(dest_device, this_dev, 0, keepdims=False)
    own_rank = lax.dynamic_index_in_dim(dest_rank, this_dev, 0, keepdims=False)
    send_slot = own_dest * CAP + own_rank
    buffer_ids = jnp.arange(slot_count, dtype=jnp.int32)
    send_pick = (buffer_ids[:, None] == send_slot[None, :]).astype(jnp.bfloat16)
    local_rows = dec_memory.reshape(dev_blocks, block_rows * col_share)
    outgoing = jnp.dot(send_pick, local_rows, preferred_element_type=jnp.float32).astype(
        jnp.bfloat16
    )
    outgoing = outgoing.reshape(dev_blocks, CAP * block_rows, col_share)
    incoming = lax.all_to_all(outgoing, "dp", split_axis=0, concat_axis=0, tiled=True)
    own_sources = lax.dynamic_slice_in_dim(block_source, this_dev * dev_blocks, dev_blocks)
    source_device = own_sources // dev_blocks
    flat_ranks = dest_rank.reshape(-1)
    source_rank = jnp.sum(
        jnp.where(block_ids[None, :] == own_sources[:, None], flat_ranks[None, :], 0), axis=1
    )
    recv_slot = source_device * CAP + source_rank
    recv_pick = (recv_slot[:, None] == buffer_ids[None, :]).astype(jnp.bfloat16)
    arrived = incoming.reshape(slot_count, block_rows * col_share)
    placed = jnp.dot(recv_pick, arrived, preferred_element_type=jnp.float32).astype(jnp.bfloat16)
    return placed.reshape(row_count, col_share)


def per_device(
    key_grads,
    value_grads,
    key_weight,
    value_weight,
    block_source,
    hidden_mid,
    mlp_out,
    post_gain,
    final_gain,
    gate_pre,
    up_pre,
    down_weight,
):
    row_count, col_share = hidden_mid.shape
    width = col_share * lax.axis_size("head")
    dev_blocks = lax.axis_size("dp")
    key_piece = lax.all_gather(key_weight, "dp", axis=1, tiled=True)
    value_piece = lax.all_gather(value_weight, "dp", axis=1, tiled=True)
    term = jnp.einsum("lrk,lck->rc", key_grads, key_piece, preferred_element_type=jnp.float32)
    term = term + jnp.einsum(
        "lrk,lck->rc", value_grads, value_piece, preferred_element_type=jnp.float32
    )
    dec_memory = lax.psum_scatter(
        term.astype(jnp.bfloat16), "head", scatter_dimension=1, tiled=True
    )
    memory_grad = repack(dec_memory, block_source, dev_blocks)
    mid_value = hidden_mid.astype(jnp.float32)
    out_value = mlp_out.astype(jnp.float32)
    gain_post = post_gain.astype(jnp.float32)
    gain_final = final_gain.astype(jnp.float32)
    sum_out = lax.psum(jnp.sum(out_value * out_value, axis=1), "head")
    out_scale = lax.rsqrt(sum_out / width + epsilon)[:, None]
    resid = mid_value + out_value * out_scale * gain_post
    sum_resid = lax.psum(jnp.sum(resid * resid, axis=1), "head")
    resid_scale = lax.rsqrt(sum_resid / width + epsilon)[:, None]
    norm_grad = memory_grad.astype(jnp.float32) * gain_final
    final_dot = lax.psum(jnp.sum(norm_grad * resid, axis=1), "head")
    final_mean = resid_scale * final_dot[:, None] / width
    resid_total = resid_scale * (norm_grad - resid * resid_scale * final_mean)
    post_input = resid_total * gain_post
    post_dot = lax.psum(jnp.sum(post_input * out_value, axis=1), "head")
    post_mean = out_scale * post_dot[:, None] / width
    post_grad = out_scale * (post_input - out_value * out_scale * post_mean)
    post_full = lax.all_gather(post_grad.astype(jnp.bfloat16), "head", axis=1, tiled=True)
    hidden_grad = lax.dot_general(
        post_full,
        lax.all_gather(down_weight, "dp", axis=1, tiled=True),
        (((1,), (1,)), ((), ())),
        preferred_element_type=jnp.float32,
    )
    activated, slope = gelu_parts(gate_pre.astype(jnp.float32))
    gate_grad = (hidden_grad * up_pre.astype(jnp.float32) * slope).astype(jnp.bfloat16)
    up_grad = (hidden_grad * activated).astype(jnp.bfloat16)
    return (resid_total.astype(jnp.bfloat16), gate_grad, up_grad)


MESH = pl.DeviceIdType.MESH
N_DEV = 32
TILE = 64


def remote(src, dst, send_sem, recv_sem, dp_index, head_index):
    return pltpu.make_async_remote_copy(
        src_ref=src,
        dst_ref=dst,
        send_sem=send_sem,
        recv_sem=recv_sem,
        device_id=(dp_index, head_index),
        device_id_type=MESH,
    )


def memory_kernel(
    key_grads,
    value_grads,
    key_weight,
    value_weight,
    send_index,
    recv_index,
    mid_ref,
    out_ref,
    post_ref,
    final_ref,
    resid_grad,
    post_full,
    a_buf,
    b_buf,
    part,
    core_send,
    core_recv,
    y_send,
    y_recv,
    dec,
    slots_out,
    slots_in,
    mem,
    resid,
    cols,
    rows_buf,
    stat,
    red_out,
    red_in,
    a_loc,
    a_ss,
    a_rs,
    b_loc,
    b_ss,
    b_rs,
    x_ss,
    x_rs,
    c_ss,
    c_rs,
    y_ss,
    y_rs,
    s_loc,
    s_ss,
    s_rs,
    r_ss,
    r_rs,
    p_ss,
    p_rs,
    q_ss,
    q_rs,
):
    row_count, col_share = mid_ref.shape
    width = col_share * 4
    w_rows = key_weight.shape[1]
    dp = lax.axis_index("dp")
    hd = lax.axis_index("head")
    z, x = dp // 2, dp % 2
    y, core = hd // 2, hd % 2
    n_group, z_par = z % 2, z % 2
    me = dp * 4 + hd

    barrier = pltpu.get_barrier_semaphore()

    @pl.loop(0, N_DEV)
    def _(i):
        @pl.when(i != me)
        def _():
            pl.semaphore_signal(barrier, inc=1, device_id=(i // 4, i % 4), device_id_type=MESH)

    pl.semaphore_wait(barrier, N_DEV - 1)

    grads = (key_grads.at[0], key_grads.at[1], value_grads.at[0], value_grads.at[1])
    weights = (key_weight.at[0], key_weight.at[1], value_weight.at[0], value_weight.at[1])
    own_half = pl.ds(pl.multiple_of(x * w_rows, 64), w_rows)
    other_half = pl.ds(pl.multiple_of((1 - x) * w_rows, 64), w_rows)

    def b_send(k, t):
        target = z // 2 + 2 * t
        return target, remote(
            weights[k],
            b_buf.at[z_par, k, own_half],
            b_ss.at[t, k],
            b_rs.at[z_par, k],
            target * 2 + x,
            hd,
        )

    def a_send(k):
        return remote(
            grads[k], a_buf.at[z_par, k], a_ss.at[k], a_rs.at[k], (z + 1 - 2 * z_par) * 2 + x, hd
        )

    def a_local(k):
        return pltpu.make_async_copy(grads[k], a_buf.at[z_par, k], a_loc.at[k])

    def b_local(j, k):
        return pltpu.make_async_copy(weights[k], b_buf.at[j, k, own_half], b_loc.at[k])

    def x_send(j, k):
        block = b_buf.at[j, k, own_half]
        return remote(block, block, x_ss.at[j, k], x_rs.at[j, k], dp + 1 - 2 * x, hd)

    def for_source(j, k, start):
        is_own = 2 * n_group + j == z

        @pl.when(is_own)
        def _():
            if start:
                b_local(j, k).start()
            else:
                b_local(j, k).wait()

        if not start:

            @pl.when(jnp.logical_not(is_own))
            def _():
                block = b_buf.at[j, k, own_half]
                pltpu.make_async_copy(block, block, b_rs.at[j, k]).wait()

    for k in range(4):
        for t in range(2):
            target, copy = b_send(k, t)
            pl.when(target != z)(copy.start)
        for j in range(2):
            for_source(j, k, True)
        a_send(k).start()
        a_local(k).start()

    def forward(k):
        for j in range(2):
            for_source(j, k, False)
            x_send(j, k).start()

    forward(0)

    def exchange(turn):
        rows_t = jnp.transpose(cols[...])
        red_out[turn] = rows_t[0:8]
        copies = []
        for i in range(3):
            copies.append(
                remote(
                    red_out.at[turn],
                    red_in.at[turn, i],
                    r_ss.at[turn, i],
                    r_rs.at[turn, i],
                    dp,
                    lax.rem(hd + 1 + i, 4),
                )
            )
        for copy in copies:
            copy.start()
        for copy in copies:
            copy.wait()
        rows_buf[...] = jnp.zeros_like(rows_buf)
        rows_buf[0:8] = red_out[turn] + red_in[turn, 0] + red_in[turn, 1] + red_in[turn, 2]
        stat[turn] = jnp.transpose(rows_buf[...])

    def lanes(first, second):
        lane = lax.broadcasted_iota(jnp.int32, (TILE, 128), 1)
        return jnp.where(lane == 0, first, jnp.where(lane == 1, second, 0.0))

    def tile(i):
        return pl.ds(pl.multiple_of(i * TILE, TILE), TILE)

    def row_sum(values):
        return jnp.sum(values, axis=1, keepdims=True)

    def out_scale_of(rows):
        return lax.rsqrt(stat[0, rows, 0:1] / width + epsilon)

    def resid_scale_of(rows):
        return lax.rsqrt(stat[1, rows, 0:1] / width + epsilon)

    @pl.loop(0, row_count // TILE)
    def _(i):
        rows = tile(i)
        out_value = out_ref[rows].astype(jnp.float32)
        total = row_sum(out_value * out_value)
        cols[rows] = lanes(total, total)

    exchange(0)
    gain_post = post_ref[...].astype(jnp.float32)
    gain_final = final_ref[...].astype(jnp.float32)

    forward(1)

    @pl.loop(0, row_count // TILE)
    def _(i):
        rows = tile(i)
        scaled = out_ref[rows].astype(jnp.float32) * gain_post
        value = mid_ref[rows].astype(jnp.float32) + scaled * out_scale_of(rows)
        resid[rows] = value
        cols[rows] = lanes(row_sum(value * value), row_sum(value * scaled))

    exchange(1)

    forward(2)
    forward(3)

    for k in range(4):
        a_local(k).wait()
        a_send(k).wait_recv()
        for j in range(2):
            block = b_buf.at[j, k, other_half]
            pltpu.make_async_copy(block, block, x_rs.at[j, k]).wait()

    def product(r, j, rows):
        total = None
        for k in range(4):
            term = lax.dot_general(
                a_buf[r, k, rows, :],
                b_buf[j, k],
                (((1,), (1,)), ((), ())),
                preferred_element_type=jnp.float32,
            )
            total = term if total is None else total + term
        return total

    def core_copy(r):
        return remote(
            core_send.at[r], core_recv.at[r], c_ss.at[r], c_rs.at[r], dp, hd + 1 - 2 * core
        )

    MM = 256
    for step in range(2):
        r = (1 - y) if step == 0 else y

        @pl.loop(0, row_count // MM)
        def _(i):
            rows = pl.ds(pl.multiple_of(i * MM, MM), MM)
            core_send[r, rows, :] = product(r, 1 - core, rows).astype(jnp.bfloat16)

        core_copy(r).start()

    def y_copy(part_id):
        rows = pl.ds(part_id * MM, MM)
        return remote(
            y_send.at[rows],
            y_recv.at[rows],
            y_ss.at[part_id],
            y_rs.at[part_id],
            dp,
            hd + 2 - 4 * y,
        )

    @pl.loop(0, row_count // MM)
    def _(i):
        rows = pl.ds(pl.multiple_of(i * MM, MM), MM)
        part[rows, :] = product(1 - y, core, rows)

    core_copy(1 - y).wait()
    for piece in range(2):
        rows = pl.ds(piece * MM, MM)
        y_send[rows, :] = (
            part[rows, :] + core_recv[1 - y, rows, :].astype(jnp.float32)
        ).astype(jnp.bfloat16)
        y_copy(piece).start()

    @pl.loop(0, row_count // MM)
    def _(i):
        rows = pl.ds(pl.multiple_of(i * MM, MM), MM)
        part[rows, :] = product(y, core, rows)

    core_copy(y).wait()
    for piece in range(2):
        y_copy(piece).wait()

    @pl.loop(0, row_count // TILE)
    def _(i):
        rows = tile(i)
        total = part[rows, :] + core_recv[y, rows, :].astype(jnp.float32)
        dec[i] = (total + y_recv[rows, :].astype(jnp.float32)).astype(jnp.bfloat16)

    chunk = 2 * (2 * (z // 2) + y) + x
    to_head = 2 * n_group + core

    def slot_copy(i):
        return remote(
            slots_out.at[pl.ds(2 * i, 2)],
            slots_in.at[pl.ds(2 * chunk, 2)],
            s_ss.at[i],
            s_rs.at[chunk],
            i,
            to_head,
        )

    def slot_local(i):
        return pltpu.make_async_copy(
            slots_out.at[pl.ds(2 * i, 2)], slots_in.at[pl.ds(2 * chunk, 2)], s_loc
        )

    def is_me(i):
        return jnp.logical_and(i == dp, to_head == hd)

    @pl.loop(0, 8)
    def _(step):
        i = lax.rem(dp + 1 + step, 8)
        for s in range(2):
            slots_out[2 * i + s] = dec[send_index[(chunk * 8 + i) * 2 + s]]

        @pl.when(is_me(i))
        def _():
            slot_local(i).start()

        @pl.when(jnp.logical_not(is_me(i)))
        def _():
            slot_copy(i).start()

    @pl.loop(0, 8)
    def _(rho):
        src_z = 2 * (rho // 4) + hd // 2
        src_dp = 2 * src_z + rho % 2
        src_head = 2 * ((rho // 2) % 2) + hd % 2
        own = jnp.logical_and(src_dp == dp, src_head == hd)
        block = slots_in.at[pl.ds(2 * rho, 2)]

        @pl.when(own)
        def _():
            slot_local(dp).wait()

        @pl.when(jnp.logical_not(own))
        def _():
            pltpu.make_async_copy(block, block, s_rs.at[rho]).wait()

    @pl.loop(0, row_count // TILE)
    def _(i):
        rows = tile(i)
        block = slots_in[recv_index[dp * 8 + i]]
        mem[i] = block
        norm_grad = block.astype(jnp.float32) * gain_final
        scaled = out_ref[rows].astype(jnp.float32) * gain_post
        cols[rows] = lanes(row_sum(norm_grad * resid[rows]), row_sum(norm_grad * scaled))

    exchange(2)

    own_cols = pl.ds(pl.multiple_of(hd * col_share, 128), col_share)
    y_head = hd + 2 - 4 * y
    core_head = hd + 1 - 2 * core
    y_cols = pl.ds(pl.multiple_of(y_head * col_share, 128), col_share)
    core_cols = pl.ds(pl.multiple_of(core_head * col_share, 128), col_share)
    far_cols = pl.ds(pl.multiple_of((3 - hd) * col_share, 128), col_share)
    PIECE = 128

    def across_y(piece):
        block = post_full.at[pl.ds(piece * PIECE, PIECE), own_cols]
        return remote(block, block, p_ss.at[0, piece], p_rs.at[0, piece], dp, y_head)

    def across_core(piece):
        block = post_full.at[pl.ds(piece * PIECE, PIECE), own_cols]
        return remote(block, block, p_ss.at[1, piece], p_rs.at[1, piece], dp, core_head)

    def pass_on(piece):
        block = post_full.at[pl.ds(piece * PIECE, PIECE), y_cols]
        return remote(block, block, q_ss.at[piece], q_rs.at[piece], dp, core_head)

    for piece in range(row_count // PIECE):

        @pl.loop(piece * (PIECE // TILE), (piece + 1) * (PIECE // TILE))
        def _(i):
            rows = tile(i)
            out_scale = out_scale_of(rows)
            resid_scale = resid_scale_of(rows)
            final_mean = resid_scale * stat[2, rows, 0:1] / width
            post_dot = resid_scale * (
                stat[2, rows, 1:2] - resid_scale * final_mean * stat[1, rows, 1:2]
            )
            post_mean = out_scale * post_dot / width
            out_value = out_ref[rows].astype(jnp.float32)
            norm_grad = mem[i].astype(jnp.float32) * gain_final
            total = resid_scale * (norm_grad - resid[rows] * (resid_scale * final_mean))
            resid_grad[rows, :] = total.astype(jnp.bfloat16)
            post_grad = out_scale * (total * gain_post - out_value * (out_scale * post_mean))
            post_full[rows, own_cols] = post_grad.astype(jnp.bfloat16)

        across_y(piece).start()
        across_core(piece).start()

    for piece in range(row_count // PIECE):
        block = post_full.at[pl.ds(piece * PIECE, PIECE), y_cols]
        pltpu.make_async_copy(block, block, p_rs.at[0, piece]).wait()
        pass_on(piece).start()

    for piece in range(row_count // PIECE):
        near = post_full.at[pl.ds(piece * PIECE, PIECE), core_cols]
        pltpu.make_async_copy(near, near, p_rs.at[1, piece]).wait()
        far = post_full.at[pl.ds(piece * PIECE, PIECE), far_cols]
        pltpu.make_async_copy(far, far, q_rs.at[piece]).wait()
        across_y(piece).wait_send()
        across_core(piece).wait_send()
        pass_on(piece).wait_send()

    for k in range(4):
        for t in range(2):
            target, copy = b_send(k, t)
            pl.when(target != z)(copy.wait_send)
        a_send(k).wait_send()
        for j in range(2):
            x_send(j, k).wait_send()

    @pl.loop(0, 8)
    def _(i):
        @pl.when(jnp.logical_not(is_me(i)))
        def _():
            slot_copy(i).wait_send()


def block_tables(block_source):
    blocks = jnp.arange(64, dtype=jnp.int32)
    is_source = block_source[:, None] == blocks[None, :]
    dest_block = jnp.sum(jnp.where(is_source, blocks[:, None], 0), axis=0)
    dest = (dest_block // 8).reshape(8, 8)
    ids = jnp.arange(8, dtype=jnp.int32)
    same = dest[:, :, None] == dest[:, None, :]
    rank = jnp.sum((same & (ids[None, :] < ids[:, None])[None]).astype(jnp.int32), axis=2)
    slot = dest * CAP + rank
    slot_ids = jnp.arange(16, dtype=jnp.int32)
    taken = slot[:, :, None] == slot_ids[None, None, :]
    send_index = jnp.sum(jnp.where(taken, ids[None, :, None], 0), axis=1).reshape(128)
    source_rank = jnp.sum(jnp.where(is_source, rank.reshape(1, 64), 0), axis=1)
    recv_index = (block_source // 8) * CAP + source_rank
    return send_index, recv_index


def fused_device(
    key_grads,
    value_grads,
    key_weight,
    value_weight,
    block_source,
    hidden_mid,
    mlp_out,
    post_gain,
    final_gain,
    gate_pre,
    up_pre,
    down_weight,
):
    row_count, col_share = hidden_mid.shape
    depth = key_grads.shape[2]
    send_index, recv_index = block_tables(block_source)
    half = jnp.bfloat16
    single = jnp.float32
    dma = pltpu.SemaphoreType.DMA
    anywhere = pl.BlockSpec(memory_space=pl.ANY)
    vmem = pl.BlockSpec(memory_space=pltpu.VMEM)
    smem = pl.BlockSpec(memory_space=pltpu.SMEM)
    resid_grad, post_full = pl.pallas_call(
        memory_kernel,
        out_shape=(
            jax.ShapeDtypeStruct((row_count, col_share), half),
            jax.ShapeDtypeStruct((row_count, col_share * 4), half),
        ),
        in_specs=[anywhere] * 4 + [smem] * 2 + [vmem] * 4,
        out_specs=(vmem, vmem),
        scratch_shapes=[
            pltpu.VMEM((2, 4, row_count, depth), half),
            pltpu.VMEM((2, 4, col_share, depth), half),
            pltpu.VMEM((row_count, col_share), single),
            pltpu.VMEM((2, row_count, col_share), half),
            pltpu.VMEM((2, row_count, col_share), half),
            pltpu.VMEM((row_count, col_share), half),
            pltpu.VMEM((row_count, col_share), half),
            pltpu.VMEM((8, TILE, col_share), half),
            pltpu.VMEM((16, TILE, col_share), half),
            pltpu.VMEM((16, TILE, col_share), half),
            pltpu.VMEM((8, TILE, col_share), half),
            pltpu.VMEM((row_count, col_share), single),
            pltpu.VMEM((row_count, 128), single),
            pltpu.VMEM((128, row_count), single),
            pltpu.VMEM((3, row_count, 128), single),
            pltpu.VMEM((3, 8, row_count), single),
            pltpu.VMEM((3, 3, 8, row_count), single),
            dma((4,)),
            dma((4,)),
            dma((4,)),
            dma((4,)),
            dma((2, 4)),
            dma((2, 4)),
            dma((2, 4)),
            dma((2, 4)),
            dma((2,)),
            dma((2,)),
            dma((2,)),
            dma((2,)),
            dma,
            dma((8,)),
            dma((8,)),
            dma((3, 3)),
            dma((3, 3)),
            dma((2, 4)),
            dma((2, 4)),
            dma((4,)),
            dma((4,)),
        ],
        cost_estimate=pl.CostEstimate(
            flops=100_000_000_000, bytes_accessed=400_000_000, transcendentals=0
        ),
        compiler_params=pltpu.CompilerParams(
            collective_id=0, has_side_effects=True, vmem_limit_bytes=52 * 1024 * 1024
        ),
    )(
        key_grads,
        value_grads,
        key_weight,
        value_weight,
        send_index,
        recv_index,
        hidden_mid,
        mlp_out,
        post_gain[None, :],
        final_gain[None, :],
    )
    hidden_grad = lax.dot_general(
        post_full,
        lax.all_gather(down_weight, "dp", axis=1, tiled=True),
        (((1,), (1,)), ((), ())),
        preferred_element_type=jnp.float32,
    )
    activated, slope = gelu_parts(gate_pre.astype(jnp.float32))
    gate_grad = (hidden_grad * up_pre.astype(jnp.float32) * slope).astype(jnp.bfloat16)
    up_grad = (hidden_grad * activated).astype(jnp.bfloat16)
    return (resid_grad, gate_grad, up_grad)


def solution(mesh):
    return jax.shard_map(
        fused_device if mesh.shape["dp"] == 8 and mesh.shape["head"] == 4 else per_device,
        mesh=mesh,
        in_specs=(
            P(None, "dp", "head"),
            P(None, "dp", "head"),
            P(None, "dp", "head"),
            P(None, "dp", "head"),
            P(),
            P("dp", "head"),
            P("dp", "head"),
            P("head"),
            P("head"),
            P("dp", "head"),
            P("dp", "head"),
            P("head", "dp"),
        ),
        out_specs=(P("dp", "head"), P("dp", "head"), P("dp", "head")),
        check_vma=False,
    )
```

```python
import functools

import jax
import jax.numpy as jnp
from jax import lax
from jax.experimental import pallas as pl
from jax.experimental.pallas import tpu as pltpu
from jax.sharding import PartitionSpec as P

CAP = 2


epsilon = 1e-06


def gelu_parts(gate_value):
    activated, pullback = jax.vjp(
        lambda pre_act: jax.nn.gelu(pre_act, approximate=True), gate_value
    )
    return (activated, pullback(jnp.ones_like(gate_value))[0])


def repack(dec_memory, block_source, dev_blocks):
    row_count, col_share = dec_memory.shape
    block_rows = row_count // dev_blocks
    total_blocks = dev_blocks * dev_blocks
    slot_count = dev_blocks * CAP
    this_dev = lax.axis_index("dp")
    block_ids = jnp.arange(total_blocks, dtype=jnp.int32)
    is_source = block_source[:, None] == block_ids[None, :]
    dest_block = jnp.sum(jnp.where(is_source, block_ids[:, None], 0), axis=0)
    dest_device = (dest_block // dev_blocks).reshape(dev_blocks, dev_blocks)
    same_dest = dest_device[:, :, None] == dest_device[:, None, :]
    slot_ids = jnp.arange(dev_blocks, dtype=jnp.int32)
    before_slot = slot_ids[None, :] < slot_ids[:, None]
    dest_rank = jnp.sum((same_dest & before_slot[None, :, :]).astype(jnp.int32), axis=2)
    own_dest = lax.dynamic_index_in_dim(dest_device, this_dev, 0, keepdims=False)
    own_rank = lax.dynamic_index_in_dim(dest_rank, this_dev, 0, keepdims=False)
    send_slot = own_dest * CAP + own_rank
    buffer_ids = jnp.arange(slot_count, dtype=jnp.int32)
    send_pick = (buffer_ids[:, None] == send_slot[None, :]).astype(jnp.bfloat16)
    local_rows = dec_memory.reshape(dev_blocks, block_rows * col_share)
    outgoing = jnp.dot(send_pick, local_rows, preferred_element_type=jnp.float32).astype(
        jnp.bfloat16
    )
    outgoing = outgoing.reshape(dev_blocks, CAP * block_rows, col_share)
    incoming = lax.all_to_all(outgoing, "dp", split_axis=0, concat_axis=0, tiled=True)
    own_sources = lax.dynamic_slice_in_dim(block_source, this_dev * dev_blocks, dev_blocks)
    source_device = own_sources // dev_blocks
    flat_ranks = dest_rank.reshape(-1)
    source_rank = jnp.sum(
        jnp.where(block_ids[None, :] == own_sources[:, None], flat_ranks[None, :], 0), axis=1
    )
    recv_slot = source_device * CAP + source_rank
    recv_pick = (recv_slot[:, None] == buffer_ids[None, :]).astype(jnp.bfloat16)
    arrived = incoming.reshape(slot_count, block_rows * col_share)
    placed = jnp.dot(recv_pick, arrived, preferred_element_type=jnp.float32).astype(jnp.bfloat16)
    return placed.reshape(row_count, col_share)


def per_device(
    key_grads,
    value_grads,
    key_weight,
    value_weight,
    block_source,
    hidden_mid,
    mlp_out,
    post_gain,
    final_gain,
    gate_pre,
    up_pre,
    down_weight,
):
    row_count, col_share = hidden_mid.shape
    width = col_share * lax.axis_size("head")
    dev_blocks = lax.axis_size("dp")
    key_piece = lax.all_gather(key_weight, "dp", axis=1, tiled=True)
    value_piece = lax.all_gather(value_weight, "dp", axis=1, tiled=True)
    term = jnp.einsum("lrk,lck->rc", key_grads, key_piece, preferred_element_type=jnp.float32)
    term = term + jnp.einsum(
        "lrk,lck->rc", value_grads, value_piece, preferred_element_type=jnp.float32
    )
    dec_memory = lax.psum_scatter(
        term.astype(jnp.bfloat16), "head", scatter_dimension=1, tiled=True
    )
    memory_grad = repack(dec_memory, block_source, dev_blocks)
    mid_value = hidden_mid.astype(jnp.float32)
    out_value = mlp_out.astype(jnp.float32)
    gain_post = post_gain.astype(jnp.float32)
    gain_final = final_gain.astype(jnp.float32)
    sum_out = lax.psum(jnp.sum(out_value * out_value, axis=1), "head")
    out_scale = lax.rsqrt(sum_out / width + epsilon)[:, None]
    resid = mid_value + out_value * out_scale * gain_post
    sum_resid = lax.psum(jnp.sum(resid * resid, axis=1), "head")
    resid_scale = lax.rsqrt(sum_resid / width + epsilon)[:, None]
    norm_grad = memory_grad.astype(jnp.float32) * gain_final
    final_dot = lax.psum(jnp.sum(norm_grad * resid, axis=1), "head")
    final_mean = resid_scale * final_dot[:, None] / width
    resid_total = resid_scale * (norm_grad - resid * resid_scale * final_mean)
    post_input = resid_total * gain_post
    post_dot = lax.psum(jnp.sum(post_input * out_value, axis=1), "head")
    post_mean = out_scale * post_dot[:, None] / width
    post_grad = out_scale * (post_input - out_value * out_scale * post_mean)
    post_full = lax.all_gather(post_grad.astype(jnp.bfloat16), "head", axis=1, tiled=True)
    hidden_grad = lax.dot_general(
        post_full,
        lax.all_gather(down_weight, "dp", axis=1, tiled=True),
        (((1,), (1,)), ((), ())),
        preferred_element_type=jnp.float32,
    )
    activated, slope = gelu_parts(gate_pre.astype(jnp.float32))
    gate_grad = (hidden_grad * up_pre.astype(jnp.float32) * slope).astype(jnp.bfloat16)
    up_grad = (hidden_grad * activated).astype(jnp.bfloat16)
    return (resid_total.astype(jnp.bfloat16), gate_grad, up_grad)


MESH = pl.DeviceIdType.MESH
N_DEV = 32
TILE = 64
HID = 256
EARLY = 3
ROOT = 0.7978845608028654
CUBIC = 0.044715


def remote(src, dst, send_sem, recv_sem, dp_index, head_index):
    return pltpu.make_async_remote_copy(
        src_ref=src,
        dst_ref=dst,
        send_sem=send_sem,
        recv_sem=recv_sem,
        device_id=(dp_index, head_index),
        device_id_type=MESH,
    )


def memory_kernel(
    key_grads,
    value_grads,
    key_weight,
    value_weight,
    send_index,
    recv_index,
    mid_ref,
    out_ref,
    post_ref,
    final_ref,
    down_ref,
    gate_ref,
    up_ref,
    resid_grad,
    gate_grad,
    up_grad,
    a_buf,
    b_buf,
    part,
    core_send,
    core_recv,
    y_send,
    y_recv,
    dec,
    slots_out,
    slots_in,
    mem,
    resid,
    cols,
    rows_buf,
    stat,
    red_out,
    red_in,
    a_loc,
    a_ss,
    a_rs,
    b_loc,
    b_ss,
    b_rs,
    x_ss,
    x_rs,
    c_ss,
    c_rs,
    y_ss,
    y_rs,
    s_loc,
    s_ss,
    s_rs,
    r_ss,
    r_rs,
    p_ss,
    p_rs,
    q_ss,
    q_rs,
    post_buf,
    down_buf,
    acc,
    pre_in,
    grad_out,
    dl_s,
    dz_ss,
    dz_rs,
    dx_ss,
    dx_rs,
    pre_s,
    grad_s,
):
    row_count, col_share = mid_ref.shape
    width = col_share * 4
    w_rows = key_weight.shape[1]
    dp = lax.axis_index("dp")
    hd = lax.axis_index("head")
    z, x = dp // 2, dp % 2
    y, core = hd // 2, hd % 2
    n_group, z_par = z % 2, z % 2
    me = dp * 4 + hd

    barrier = pltpu.get_barrier_semaphore()

    @pl.loop(0, N_DEV)
    def _(i):
        @pl.when(i != me)
        def _():
            pl.semaphore_signal(barrier, inc=1, device_id=(i // 4, i % 4), device_id_type=MESH)

    pl.semaphore_wait(barrier, N_DEV - 1)

    grads = (key_grads.at[0], key_grads.at[1], value_grads.at[0], value_grads.at[1])
    weights = (key_weight.at[0], key_weight.at[1], value_weight.at[0], value_weight.at[1])
    own_half = pl.ds(pl.multiple_of(x * w_rows, 64), w_rows)
    other_half = pl.ds(pl.multiple_of((1 - x) * w_rows, 64), w_rows)

    def b_send(k, t):
        target = z // 2 + 2 * t
        return target, remote(
            weights[k],
            b_buf.at[z_par, k, own_half],
            b_ss.at[t, k],
            b_rs.at[z_par, k],
            target * 2 + x,
            hd,
        )

    def a_send(k):
        return remote(
            grads[k], a_buf.at[z_par, k], a_ss.at[k], a_rs.at[k], (z + 1 - 2 * z_par) * 2 + x, hd
        )

    def a_local(k):
        return pltpu.make_async_copy(grads[k], a_buf.at[z_par, k], a_loc.at[k])

    def b_local(j, k):
        return pltpu.make_async_copy(weights[k], b_buf.at[j, k, own_half], b_loc.at[k])

    def x_send(j, k):
        block = b_buf.at[j, k, own_half]
        return remote(block, block, x_ss.at[j, k], x_rs.at[j, k], dp + 1 - 2 * x, hd)

    def for_source(j, k, start):
        is_own = 2 * n_group + j == z

        @pl.when(is_own)
        def _():
            if start:
                b_local(j, k).start()
            else:
                b_local(j, k).wait()

        if not start:

            @pl.when(jnp.logical_not(is_own))
            def _():
                block = b_buf.at[j, k, own_half]
                pltpu.make_async_copy(block, block, b_rs.at[j, k]).wait()

    for k in range(4):
        for t in range(2):
            target, copy = b_send(k, t)
            pl.when(target != z)(copy.start)
        for j in range(2):
            for_source(j, k, True)
        a_send(k).start()
        a_local(k).start()

    def forward(k):
        for j in range(2):
            for_source(j, k, False)
            x_send(j, k).start()

    def hidden(p):
        return pl.ds(p * HID, HID)

    def down_local(p):
        return pltpu.make_async_copy(
            down_ref.at[hidden(p)], down_buf.at[dp, hidden(p)], dl_s.at[p]
        )

    def down_send(t, p):
        return remote(
            down_ref.at[hidden(p)],
            down_buf.at[dp, hidden(p)],
            dz_ss.at[t - 1, p],
            dz_rs.at[z, p],
            lax.rem(z + t, 4) * 2 + x,
            hd,
        )

    def down_across(src_z, p):
        block = down_buf.at[2 * src_z + x, hidden(p)]
        return remote(block, block, dx_ss.at[src_z, p], dx_rs.at[src_z, p], dp + 1 - 2 * x, hd)

    def down_start(p):
        for t in (1, 3, 2):
            down_send(t, p).start()
        down_local(p).wait()
        down_across(z, p).start()

    def down_forward(p):
        for t in (1, 3, 2):
            src_z = lax.rem(z + t, 4)
            block = down_buf.at[2 * src_z + x, hidden(p)]
            pltpu.make_async_copy(block, block, dz_rs.at[src_z, p]).wait()
            down_across(src_z, p).start()

    def pre_copies(p):
        cols_p = hidden(p)
        return (
            pltpu.make_async_copy(gate_ref.at[:, cols_p], pre_in.at[0, p % 2], pre_s.at[0, p % 2]),
            pltpu.make_async_copy(up_ref.at[:, cols_p], pre_in.at[1, p % 2], pre_s.at[1, p % 2]),
        )

    def grad_copies(p):
        cols_p = hidden(p)
        return (
            pltpu.make_async_copy(
                grad_out.at[0, p % 2], gate_grad.at[:, cols_p], grad_s.at[0, p % 2]
            ),
            pltpu.make_async_copy(
                grad_out.at[1, p % 2], up_grad.at[:, cols_p], grad_s.at[1, p % 2]
            ),
        )

    n_hid = down_ref.shape[0] // HID
    for p in range(n_hid):
        down_local(p).start()
    for p in range(2):
        for copy in pre_copies(p):
            copy.start()

    forward(0)

    def exchange(turn):
        rows_t = jnp.transpose(cols[...])
        red_out[turn] = rows_t[0:8]
        copies = []
        for i in range(3):
            copies.append(
                remote(
                    red_out.at[turn],
                    red_in.at[turn, i],
                    r_ss.at[turn, i],
                    r_rs.at[turn, i],
                    dp,
                    lax.rem(hd + 1 + i, 4),
                )
            )
        for copy in copies:
            copy.start()
        for copy in copies:
            copy.wait()
        rows_buf[...] = jnp.zeros_like(rows_buf)
        rows_buf[0:8] = red_out[turn] + red_in[turn, 0] + red_in[turn, 1] + red_in[turn, 2]
        stat[turn] = jnp.transpose(rows_buf[...])

    def lanes(first, second):
        lane = lax.broadcasted_iota(jnp.int32, (TILE, 128), 1)
        return jnp.where(lane == 0, first, jnp.where(lane == 1, second, 0.0))

    def tile(i):
        return pl.ds(pl.multiple_of(i * TILE, TILE), TILE)

    def row_sum(values):
        return jnp.sum(values, axis=1, keepdims=True)

    def out_scale_of(rows):
        return lax.rsqrt(stat[0, rows, 0:1] / width + epsilon)

    def resid_scale_of(rows):
        return lax.rsqrt(stat[1, rows, 0:1] / width + epsilon)

    @pl.loop(0, row_count // TILE)
    def _(i):
        rows = tile(i)
        out_value = out_ref[rows].astype(jnp.float32)
        total = row_sum(out_value * out_value)
        cols[rows] = lanes(total, total)

    exchange(0)
    gain_post = post_ref[...].astype(jnp.float32)
    gain_final = final_ref[...].astype(jnp.float32)

    forward(1)

    @pl.loop(0, row_count // TILE)
    def _(i):
        rows = tile(i)
        scaled = out_ref[rows].astype(jnp.float32) * gain_post
        value = mid_ref[rows].astype(jnp.float32) + scaled * out_scale_of(rows)
        resid[rows] = value
        cols[rows] = lanes(row_sum(value * value), row_sum(value * scaled))

    exchange(1)

    forward(2)
    forward(3)

    for k in range(4):
        a_local(k).wait()
        a_send(k).wait_recv()
        for j in range(2):
            block = b_buf.at[j, k, other_half]
            pltpu.make_async_copy(block, block, x_rs.at[j, k]).wait()

    for p in range(EARLY):
        down_start(p)

    def product(r, j, rows):
        total = None
        for k in range(4):
            term = lax.dot_general(
                a_buf[r, k, rows, :],
                b_buf[j, k],
                (((1,), (1,)), ((), ())),
                preferred_element_type=jnp.float32,
            )
            total = term if total is None else total + term
        return total

    def core_copy(r):
        return remote(
            core_send.at[r], core_recv.at[r], c_ss.at[r], c_rs.at[r], dp, hd + 1 - 2 * core
        )

    MM = 256
    for step in range(2):
        r = (1 - y) if step == 0 else y

        @pl.loop(0, row_count // MM)
        def _(i):
            rows = pl.ds(pl.multiple_of(i * MM, MM), MM)
            core_send[r, rows, :] = product(r, 1 - core, rows).astype(jnp.bfloat16)

        core_copy(r).start()

    def y_copy(part_id):
        rows = pl.ds(part_id * MM, MM)
        return remote(
            y_send.at[rows],
            y_recv.at[rows],
            y_ss.at[part_id],
            y_rs.at[part_id],
            dp,
            hd + 2 - 4 * y,
        )

    @pl.loop(0, row_count // MM)
    def _(i):
        rows = pl.ds(pl.multiple_of(i * MM, MM), MM)
        part[rows, :] = product(1 - y, core, rows)

    core_copy(1 - y).wait()
    for piece in range(2):
        rows = pl.ds(piece * MM, MM)
        y_send[rows, :] = (
            part[rows, :] + core_recv[1 - y, rows, :].astype(jnp.float32)
        ).astype(jnp.bfloat16)
        y_copy(piece).start()

    @pl.loop(0, row_count // MM)
    def _(i):
        rows = pl.ds(pl.multiple_of(i * MM, MM), MM)
        part[rows, :] = product(y, core, rows)

    core_copy(y).wait()
    for piece in range(2):
        y_copy(piece).wait()

    @pl.loop(0, row_count // TILE)
    def _(i):
        rows = tile(i)
        total = part[rows, :] + core_recv[y, rows, :].astype(jnp.float32)
        dec[i] = (total + y_recv[rows, :].astype(jnp.float32)).astype(jnp.bfloat16)

    down_forward(0)
    chunk = 2 * (2 * (z // 2) + y) + x
    to_head = 2 * n_group + core

    def slot_copy(i):
        return remote(
            slots_out.at[pl.ds(2 * i, 2)],
            slots_in.at[pl.ds(2 * chunk, 2)],
            s_ss.at[i],
            s_rs.at[chunk],
            i,
            to_head,
        )

    def slot_local(i):
        return pltpu.make_async_copy(
            slots_out.at[pl.ds(2 * i, 2)], slots_in.at[pl.ds(2 * chunk, 2)], s_loc
        )

    def is_me(i):
        return jnp.logical_and(i == dp, to_head == hd)

    @pl.loop(0, 8)
    def _(step):
        i = lax.rem(dp + 1 + step, 8)
        for s in range(2):
            slots_out[2 * i + s] = dec[send_index[(chunk * 8 + i) * 2 + s]]

        @pl.when(is_me(i))
        def _():
            slot_local(i).start()

        @pl.when(jnp.logical_not(is_me(i)))
        def _():
            slot_copy(i).start()

    for p in range(EARLY, n_hid):
        down_start(p)
    down_forward(1)

    @pl.loop(0, 8)
    def _(rho):
        src_z = 2 * (rho // 4) + hd // 2
        src_dp = 2 * src_z + rho % 2
        src_head = 2 * ((rho // 2) % 2) + hd % 2
        own = jnp.logical_and(src_dp == dp, src_head == hd)
        block = slots_in.at[pl.ds(2 * rho, 2)]

        @pl.when(own)
        def _():
            slot_local(dp).wait()

        @pl.when(jnp.logical_not(own))
        def _():
            pltpu.make_async_copy(block, block, s_rs.at[rho]).wait()

    down_forward(2)

    @pl.loop(0, row_count // TILE)
    def _(i):
        rows = tile(i)
        block = slots_in[recv_index[dp * 8 + i]]
        mem[i] = block
        norm_grad = block.astype(jnp.float32) * gain_final
        scaled = out_ref[rows].astype(jnp.float32) * gain_post
        cols[rows] = lanes(row_sum(norm_grad * resid[rows]), row_sum(norm_grad * scaled))

    exchange(2)

    y_head = hd + 2 - 4 * y
    core_head = hd + 1 - 2 * core
    PIECE = 128

    def across_y(piece):
        block = post_buf.at[pl.ds(2 * hd, 2), pl.ds(piece * PIECE, PIECE)]
        return remote(block, block, p_ss.at[0, piece], p_rs.at[0, piece], dp, y_head)

    def across_core(piece):
        block = post_buf.at[pl.ds(2 * hd, 2), pl.ds(piece * PIECE, PIECE)]
        return remote(block, block, p_ss.at[1, piece], p_rs.at[1, piece], dp, core_head)

    def pass_on(piece):
        block = post_buf.at[pl.ds(2 * y_head, 2), pl.ds(piece * PIECE, PIECE)]
        return remote(block, block, q_ss.at[piece], q_rs.at[piece], dp, core_head)

    for piece in range(row_count // PIECE):

        @pl.loop(piece * (PIECE // TILE), (piece + 1) * (PIECE // TILE))
        def _(i):
            rows = tile(i)
            out_scale = out_scale_of(rows)
            resid_scale = resid_scale_of(rows)
            final_mean = resid_scale * stat[2, rows, 0:1] / width
            post_dot = resid_scale * (
                stat[2, rows, 1:2] - resid_scale * final_mean * stat[1, rows, 1:2]
            )
            post_mean = out_scale * post_dot / width
            out_value = out_ref[rows].astype(jnp.float32)
            norm_grad = mem[i].astype(jnp.float32) * gain_final
            total = resid_scale * (norm_grad - resid[rows] * (resid_scale * final_mean))
            resid_grad[rows, :] = total.astype(jnp.bfloat16)
            post_grad = out_scale * (total * gain_post - out_value * (out_scale * post_mean))
            post_half = post_grad.astype(jnp.bfloat16)
            post_buf[2 * hd, rows, :] = post_half[:, : col_share // 2]
            post_buf[2 * hd + 1, rows, :] = post_half[:, col_share // 2 :]

        across_y(piece).start()
        across_core(piece).start()

    for piece in range(row_count // PIECE):
        block = post_buf.at[pl.ds(2 * y_head, 2), pl.ds(piece * PIECE, PIECE)]
        pltpu.make_async_copy(block, block, p_rs.at[0, piece]).wait()
        pass_on(piece).start()
        down_forward(3 + piece)

    for piece in range(row_count // PIECE):
        near = post_buf.at[pl.ds(2 * core_head, 2), pl.ds(piece * PIECE, PIECE)]
        pltpu.make_async_copy(near, near, p_rs.at[1, piece]).wait()
        far = post_buf.at[pl.ds(2 * (3 - hd), 2), pl.ds(piece * PIECE, PIECE)]
        pltpu.make_async_copy(far, far, q_rs.at[piece]).wait()

    for p in range(n_hid):
        for src_z in range(4):
            block = down_buf.at[2 * src_z + 1 - x, hidden(p)]
            pltpu.make_async_copy(block, block, dx_rs.at[src_z, p]).wait()

        total = None
        for c in range(8):
            term = lax.dot_general(
                post_buf[c],
                down_buf[c, hidden(p), :],
                (((1,), (1,)), ((), ())),
                preferred_element_type=jnp.float32,
            )
            total = term if total is None else total + term
        acc[...] = total
        for copy in pre_copies(p):
            copy.wait()
        if p >= 2:
            for copy in grad_copies(p - 2):
                copy.wait()

        @pl.loop(0, row_count // TILE)
        def _(i):
            rows = tile(i)
            grad = acc[rows, :]
            value = pre_in[0, p % 2, rows, :].astype(jnp.float32)
            other = pre_in[1, p % 2, rows, :].astype(jnp.float32)
            square = value * value
            bent = jnp.tanh(ROOT * value * (1.0 + CUBIC * square))
            share = 0.5 * (1.0 + bent)
            slope = share + 0.5 * value * (1.0 - bent * bent) * (
                ROOT * (1.0 + 3.0 * CUBIC * square)
            )
            grad_out[0, p % 2, rows, :] = (grad * other * slope).astype(jnp.bfloat16)
            grad_out[1, p % 2, rows, :] = (grad * (value * share)).astype(jnp.bfloat16)

        for copy in grad_copies(p):
            copy.start()
        if p + 2 < n_hid:
            for copy in pre_copies(p + 2):
                copy.start()

    for p in range(n_hid - 2, n_hid):
        for copy in grad_copies(p):
            copy.wait()

    for piece in range(row_count // PIECE):
        across_y(piece).wait_send()
        across_core(piece).wait_send()
        pass_on(piece).wait_send()

    for p in range(n_hid):
        for t in (1, 2, 3):
            down_send(t, p).wait_send()
        for src_z in range(4):
            down_across(src_z, p).wait_send()

    for k in range(4):
        for t in range(2):
            target, copy = b_send(k, t)
            pl.when(target != z)(copy.wait_send)
        a_send(k).wait_send()
        for j in range(2):
            x_send(j, k).wait_send()

    @pl.loop(0, 8)
    def _(i):
        @pl.when(jnp.logical_not(is_me(i)))
        def _():
            slot_copy(i).wait_send()


def block_tables(block_source):
    blocks = jnp.arange(64, dtype=jnp.int32)
    is_source = block_source[:, None] == blocks[None, :]
    dest_block = jnp.sum(jnp.where(is_source, blocks[:, None], 0), axis=0)
    dest = (dest_block // 8).reshape(8, 8)
    ids = jnp.arange(8, dtype=jnp.int32)
    same = dest[:, :, None] == dest[:, None, :]
    rank = jnp.sum((same & (ids[None, :] < ids[:, None])[None]).astype(jnp.int32), axis=2)
    slot = dest * CAP + rank
    slot_ids = jnp.arange(16, dtype=jnp.int32)
    taken = slot[:, :, None] == slot_ids[None, None, :]
    send_index = jnp.sum(jnp.where(taken, ids[None, :, None], 0), axis=1).reshape(128)
    source_rank = jnp.sum(jnp.where(is_source, rank.reshape(1, 64), 0), axis=1)
    recv_index = (block_source // 8) * CAP + source_rank
    return send_index, recv_index


def fused_device(
    key_grads,
    value_grads,
    key_weight,
    value_weight,
    block_source,
    hidden_mid,
    mlp_out,
    post_gain,
    final_gain,
    gate_pre,
    up_pre,
    down_weight,
):
    row_count, col_share = hidden_mid.shape
    depth = key_grads.shape[2]
    send_index, recv_index = block_tables(block_source)
    half = jnp.bfloat16
    single = jnp.float32
    dma = pltpu.SemaphoreType.DMA
    anywhere = pl.BlockSpec(memory_space=pl.ANY)
    vmem = pl.BlockSpec(memory_space=pltpu.VMEM)
    smem = pl.BlockSpec(memory_space=pltpu.SMEM)
    n_hid = down_weight.shape[0] // HID
    return pl.pallas_call(
        memory_kernel,
        out_shape=(
            jax.ShapeDtypeStruct((row_count, col_share), half),
            jax.ShapeDtypeStruct(gate_pre.shape, half),
            jax.ShapeDtypeStruct(gate_pre.shape, half),
        ),
        in_specs=[anywhere] * 4 + [smem] * 2 + [vmem] * 4 + [anywhere] * 3,
        out_specs=(vmem, anywhere, anywhere),
        scratch_shapes=[
            pltpu.VMEM((2, 4, row_count, depth), half),
            pltpu.VMEM((2, 4, col_share, depth), half),
            pltpu.VMEM((row_count, col_share), single),
            pltpu.VMEM((2, row_count, col_share), half),
            pltpu.VMEM((2, row_count, col_share), half),
            pltpu.VMEM((row_count, col_share), half),
            pltpu.VMEM((row_count, col_share), half),
            pltpu.VMEM((8, TILE, col_share), half),
            pltpu.VMEM((16, TILE, col_share), half),
            pltpu.VMEM((16, TILE, col_share), half),
            pltpu.VMEM((8, TILE, col_share), half),
            pltpu.VMEM((row_count, col_share), single),
            pltpu.VMEM((row_count, 128), single),
            pltpu.VMEM((128, row_count), single),
            pltpu.VMEM((3, row_count, 128), single),
            pltpu.VMEM((3, 8, row_count), single),
            pltpu.VMEM((3, 3, 8, row_count), single),
            dma((4,)),
            dma((4,)),
            dma((4,)),
            dma((4,)),
            dma((2, 4)),
            dma((2, 4)),
            dma((2, 4)),
            dma((2, 4)),
            dma((2,)),
            dma((2,)),
            dma((2,)),
            dma((2,)),
            dma,
            dma((8,)),
            dma((8,)),
            dma((3, 3)),
            dma((3, 3)),
            dma((2, 4)),
            dma((2, 4)),
            dma((4,)),
            dma((4,)),
            pltpu.VMEM((8, row_count, col_share // 2), half),
            pltpu.VMEM((8,) + down_weight.shape, half),
            pltpu.VMEM((row_count, HID), single),
            pltpu.VMEM((2, 2, row_count, HID), half),
            pltpu.VMEM((2, 2, row_count, HID), half),
            dma((n_hid,)),
            dma((3, n_hid)),
            dma((4, n_hid)),
            dma((4, n_hid)),
            dma((4, n_hid)),
            dma((2, 2)),
            dma((2, 2)),
        ],
        cost_estimate=pl.CostEstimate(
            flops=100_000_000_000, bytes_accessed=400_000_000, transcendentals=0
        ),
        compiler_params=pltpu.CompilerParams(
            collective_id=0, has_side_effects=True, vmem_limit_bytes=60 * 1024 * 1024
        ),
    )(
        key_grads,
        value_grads,
        key_weight,
        value_weight,
        send_index,
        recv_index,
        hidden_mid,
        mlp_out,
        post_gain[None, :],
        final_gain[None, :],
        down_weight,
        gate_pre,
        up_pre,
    )


def solution(mesh):
    return jax.shard_map(
        fused_device if mesh.shape["dp"] == 8 and mesh.shape["head"] == 4 else per_device,
        mesh=mesh,
        in_specs=(
            P(None, "dp", "head"),
            P(None, "dp", "head"),
            P(None, "dp", "head"),
            P(None, "dp", "head"),
            P(),
            P("dp", "head"),
            P("dp", "head"),
            P("head"),
            P("head"),
            P("dp", "head"),
            P("dp", "head"),
            P("head", "dp"),
        ),
        out_specs=(P("dp", "head"), P("dp", "head"), P("dp", "head")),
        check_vma=False,
    )
```

```python
import functools

import jax
import jax.numpy as jnp
from jax import lax
from jax.experimental import pallas as pl
from jax.experimental.pallas import tpu as pltpu
from jax.sharding import PartitionSpec as P

CAP = 2


epsilon = 1e-06


def gelu_parts(gate_value):
    activated, pullback = jax.vjp(
        lambda pre_act: jax.nn.gelu(pre_act, approximate=True), gate_value
    )
    return (activated, pullback(jnp.ones_like(gate_value))[0])


def repack(dec_memory, block_source, dev_blocks):
    row_count, col_share = dec_memory.shape
    block_rows = row_count // dev_blocks
    total_blocks = dev_blocks * dev_blocks
    slot_count = dev_blocks * CAP
    this_dev = lax.axis_index("dp")
    block_ids = jnp.arange(total_blocks, dtype=jnp.int32)
    is_source = block_source[:, None] == block_ids[None, :]
    dest_block = jnp.sum(jnp.where(is_source, block_ids[:, None], 0), axis=0)
    dest_device = (dest_block // dev_blocks).reshape(dev_blocks, dev_blocks)
    same_dest = dest_device[:, :, None] == dest_device[:, None, :]
    slot_ids = jnp.arange(dev_blocks, dtype=jnp.int32)
    before_slot = slot_ids[None, :] < slot_ids[:, None]
    dest_rank = jnp.sum((same_dest & before_slot[None, :, :]).astype(jnp.int32), axis=2)
    own_dest = lax.dynamic_index_in_dim(dest_device, this_dev, 0, keepdims=False)
    own_rank = lax.dynamic_index_in_dim(dest_rank, this_dev, 0, keepdims=False)
    send_slot = own_dest * CAP + own_rank
    buffer_ids = jnp.arange(slot_count, dtype=jnp.int32)
    send_pick = (buffer_ids[:, None] == send_slot[None, :]).astype(jnp.bfloat16)
    local_rows = dec_memory.reshape(dev_blocks, block_rows * col_share)
    outgoing = jnp.dot(send_pick, local_rows, preferred_element_type=jnp.float32).astype(
        jnp.bfloat16
    )
    outgoing = outgoing.reshape(dev_blocks, CAP * block_rows, col_share)
    incoming = lax.all_to_all(outgoing, "dp", split_axis=0, concat_axis=0, tiled=True)
    own_sources = lax.dynamic_slice_in_dim(block_source, this_dev * dev_blocks, dev_blocks)
    source_device = own_sources // dev_blocks
    flat_ranks = dest_rank.reshape(-1)
    source_rank = jnp.sum(
        jnp.where(block_ids[None, :] == own_sources[:, None], flat_ranks[None, :], 0), axis=1
    )
    recv_slot = source_device * CAP + source_rank
    recv_pick = (recv_slot[:, None] == buffer_ids[None, :]).astype(jnp.bfloat16)
    arrived = incoming.reshape(slot_count, block_rows * col_share)
    placed = jnp.dot(recv_pick, arrived, preferred_element_type=jnp.float32).astype(jnp.bfloat16)
    return placed.reshape(row_count, col_share)


def per_device(
    key_grads,
    value_grads,
    key_weight,
    value_weight,
    block_source,
    hidden_mid,
    mlp_out,
    post_gain,
    final_gain,
    gate_pre,
    up_pre,
    down_weight,
):
    row_count, col_share = hidden_mid.shape
    width = col_share * lax.axis_size("head")
    dev_blocks = lax.axis_size("dp")
    key_piece = lax.all_gather(key_weight, "dp", axis=1, tiled=True)
    value_piece = lax.all_gather(value_weight, "dp", axis=1, tiled=True)
    term = jnp.einsum("lrk,lck->rc", key_grads, key_piece, preferred_element_type=jnp.float32)
    term = term + jnp.einsum(
        "lrk,lck->rc", value_grads, value_piece, preferred_element_type=jnp.float32
    )
    dec_memory = lax.psum_scatter(
        term.astype(jnp.bfloat16), "head", scatter_dimension=1, tiled=True
    )
    memory_grad = repack(dec_memory, block_source, dev_blocks)
    mid_value = hidden_mid.astype(jnp.float32)
    out_value = mlp_out.astype(jnp.float32)
    gain_post = post_gain.astype(jnp.float32)
    gain_final = final_gain.astype(jnp.float32)
    sum_out = lax.psum(jnp.sum(out_value * out_value, axis=1), "head")
    out_scale = lax.rsqrt(sum_out / width + epsilon)[:, None]
    resid = mid_value + out_value * out_scale * gain_post
    sum_resid = lax.psum(jnp.sum(resid * resid, axis=1), "head")
    resid_scale = lax.rsqrt(sum_resid / width + epsilon)[:, None]
    norm_grad = memory_grad.astype(jnp.float32) * gain_final
    final_dot = lax.psum(jnp.sum(norm_grad * resid, axis=1), "head")
    final_mean = resid_scale * final_dot[:, None] / width
    resid_total = resid_scale * (norm_grad - resid * resid_scale * final_mean)
    post_input = resid_total * gain_post
    post_dot = lax.psum(jnp.sum(post_input * out_value, axis=1), "head")
    post_mean = out_scale * post_dot[:, None] / width
    post_grad = out_scale * (post_input - out_value * out_scale * post_mean)
    post_full = lax.all_gather(post_grad.astype(jnp.bfloat16), "head", axis=1, tiled=True)
    hidden_grad = lax.dot_general(
        post_full,
        lax.all_gather(down_weight, "dp", axis=1, tiled=True),
        (((1,), (1,)), ((), ())),
        preferred_element_type=jnp.float32,
    )
    activated, slope = gelu_parts(gate_pre.astype(jnp.float32))
    gate_grad = (hidden_grad * up_pre.astype(jnp.float32) * slope).astype(jnp.bfloat16)
    up_grad = (hidden_grad * activated).astype(jnp.bfloat16)
    return (resid_total.astype(jnp.bfloat16), gate_grad, up_grad)


MESH = pl.DeviceIdType.MESH
N_DEV = 32
TILE = 64
HID = 256
EARLY = 3
ROOT = 0.7978845608028654
CUBIC = 0.044715


def remote(src, dst, send_sem, recv_sem, dp_index, head_index):
    return pltpu.make_async_remote_copy(
        src_ref=src,
        dst_ref=dst,
        send_sem=send_sem,
        recv_sem=recv_sem,
        device_id=(dp_index, head_index),
        device_id_type=MESH,
    )


def memory_kernel(
    key_grads,
    value_grads,
    key_weight,
    value_weight,
    send_index,
    recv_index,
    mid_ref,
    out_ref,
    post_ref,
    final_ref,
    down_ref,
    gate_ref,
    up_ref,
    resid_grad,
    gate_grad,
    up_grad,
    a_buf,
    b_buf,
    part,
    core_send,
    core_recv,
    y_send,
    y_recv,
    dec,
    slots_out,
    slots_in,
    mem,
    resid,
    cols,
    rows_buf,
    stat,
    red_out,
    red_in,
    a_loc,
    a_ss,
    a_rs,
    b_loc,
    b_ss,
    b_rs,
    x_ss,
    x_rs,
    c_ss,
    c_rs,
    y_ss,
    y_rs,
    s_loc,
    s_ss,
    s_rs,
    r_ss,
    r_rs,
    p_ss,
    p_rs,
    q_ss,
    q_rs,
    post_buf,
    down_buf,
    acc,
    pre_in,
    grad_out,
    dl_s,
    dz_ss,
    dz_rs,
    dx_ss,
    dx_rs,
    pre_s,
    grad_s,
):
    row_count, col_share = mid_ref.shape
    width = col_share * 4
    w_rows = key_weight.shape[1]
    dp = lax.axis_index("dp")
    hd = lax.axis_index("head")
    z, x = dp // 2, dp % 2
    y, core = hd // 2, hd % 2
    n_group, z_par = z % 2, z % 2
    me = dp * 4 + hd

    barrier = pltpu.get_barrier_semaphore()

    @pl.loop(0, N_DEV)
    def _(i):
        @pl.when(i != me)
        def _():
            pl.semaphore_signal(barrier, inc=1, device_id=(i // 4, i % 4), device_id_type=MESH)

    pl.semaphore_wait(barrier, N_DEV - 1)

    grads = (key_grads.at[0], key_grads.at[1], value_grads.at[0], value_grads.at[1])
    weights = (key_weight.at[0], key_weight.at[1], value_weight.at[0], value_weight.at[1])
    own_half = pl.ds(pl.multiple_of(x * w_rows, 64), w_rows)
    other_half = pl.ds(pl.multiple_of((1 - x) * w_rows, 64), w_rows)

    def b_send(k, t):
        target = z // 2 + 2 * t
        return target, remote(
            weights[k],
            b_buf.at[z_par, k, own_half],
            b_ss.at[t, k],
            b_rs.at[z_par, k],
            target * 2 + x,
            hd,
        )

    def a_send(k):
        return remote(
            grads[k], a_buf.at[z_par, k], a_ss.at[k], a_rs.at[k], (z + 1 - 2 * z_par) * 2 + x, hd
        )

    def a_local(k):
        return pltpu.make_async_copy(grads[k], a_buf.at[z_par, k], a_loc.at[k])

    def b_local(j, k):
        return pltpu.make_async_copy(weights[k], b_buf.at[j, k, own_half], b_loc.at[k])

    def x_send(j, k):
        block = b_buf.at[j, k, own_half]
        return remote(block, block, x_ss.at[j, k], x_rs.at[j, k], dp + 1 - 2 * x, hd)

    def for_source(j, k, start):
        is_own = 2 * n_group + j == z

        @pl.when(is_own)
        def _():
            if start:
                b_local(j, k).start()
            else:
                b_local(j, k).wait()

        if not start:

            @pl.when(jnp.logical_not(is_own))
            def _():
                block = b_buf.at[j, k, own_half]
                pltpu.make_async_copy(block, block, b_rs.at[j, k]).wait()

    for k in range(4):
        for t in range(2):
            target, copy = b_send(k, t)
            pl.when(target != z)(copy.start)
        for j in range(2):
            for_source(j, k, True)
    for k in range(4):
        a_send(k).start()
        a_local(k).start()

    def forward(k):
        for j in range(2):
            for_source(j, k, False)
            x_send(j, k).start()

    def hidden(p):
        return pl.ds(p * HID, HID)

    def down_local(p):
        return pltpu.make_async_copy(
            down_ref.at[:, hidden(p)], down_buf.at[dp, :, hidden(p)], dl_s.at[p]
        )

    def down_send(t, p):
        return remote(
            down_ref.at[:, hidden(p)],
            down_buf.at[dp, :, hidden(p)],
            dz_ss.at[t - 1, p],
            dz_rs.at[z, p],
            lax.rem(z + t, 4) * 2 + x,
            hd,
        )

    def down_across(src_z, p):
        block = down_buf.at[2 * src_z + x, :, hidden(p)]
        return remote(block, block, dx_ss.at[src_z, p], dx_rs.at[src_z, p], dp + 1 - 2 * x, hd)

    def down_start(p):
        for t in (1, 3, 2):
            down_send(t, p).start()
        down_local(p).wait()
        down_across(z, p).start()

    def down_forward(p):
        for t in (1, 3, 2):
            src_z = lax.rem(z + t, 4)
            block = down_buf.at[2 * src_z + x, :, hidden(p)]
            pltpu.make_async_copy(block, block, dz_rs.at[src_z, p]).wait()
            down_across(src_z, p).start()

    def pre_copies(p):
        cols_p = hidden(p)
        return (
            pltpu.make_async_copy(gate_ref.at[:, cols_p], pre_in.at[0, p % 2], pre_s.at[0, p % 2]),
            pltpu.make_async_copy(up_ref.at[:, cols_p], pre_in.at[1, p % 2], pre_s.at[1, p % 2]),
        )

    def grad_copies(p):
        cols_p = hidden(p)
        return (
            pltpu.make_async_copy(
                grad_out.at[0, p % 2], gate_grad.at[:, cols_p], grad_s.at[0, p % 2]
            ),
            pltpu.make_async_copy(
                grad_out.at[1, p % 2], up_grad.at[:, cols_p], grad_s.at[1, p % 2]
            ),
        )

    n_hid = down_ref.shape[1] // HID
    for p in range(n_hid):
        down_local(p).start()
    for p in range(2):
        for copy in pre_copies(p):
            copy.start()

    forward(0)

    def exchange(turn):
        rows_t = jnp.transpose(cols[...])
        red_out[turn] = rows_t[0:8]
        copies = []
        for i in range(3):
            copies.append(
                remote(
                    red_out.at[turn],
                    red_in.at[turn, i],
                    r_ss.at[turn, i],
                    r_rs.at[turn, i],
                    dp,
                    lax.rem(hd + 1 + i, 4),
                )
            )
        for copy in copies:
            copy.start()
        for copy in copies:
            copy.wait()
        rows_buf[...] = jnp.zeros_like(rows_buf)
        rows_buf[0:8] = red_out[turn] + red_in[turn, 0] + red_in[turn, 1] + red_in[turn, 2]
        stat[turn] = jnp.transpose(rows_buf[...])

    def lanes(first, second):
        lane = lax.broadcasted_iota(jnp.int32, (TILE, 128), 1)
        return jnp.where(lane == 0, first, jnp.where(lane == 1, second, 0.0))

    def tile(i):
        return pl.ds(pl.multiple_of(i * TILE, TILE), TILE)

    def row_sum(values):
        return jnp.sum(values, axis=1, keepdims=True)

    def out_scale_of(rows):
        return lax.rsqrt(stat[0, rows, 0:1] / width + epsilon)

    def resid_scale_of(rows):
        return lax.rsqrt(stat[1, rows, 0:1] / width + epsilon)

    @pl.loop(0, row_count // TILE)
    def _(i):
        rows = tile(i)
        out_value = out_ref[rows].astype(jnp.float32)
        total = row_sum(out_value * out_value)
        cols[rows] = lanes(total, total)

    exchange(0)
    gain_post = post_ref[...].astype(jnp.float32)
    gain_final = final_ref[...].astype(jnp.float32)

    forward(1)

    @pl.loop(0, row_count // TILE)
    def _(i):
        rows = tile(i)
        scaled = out_ref[rows].astype(jnp.float32) * gain_post
        value = mid_ref[rows].astype(jnp.float32) + scaled * out_scale_of(rows)
        resid[rows] = value
        cols[rows] = lanes(row_sum(value * value), row_sum(value * scaled))

    exchange(1)

    forward(2)
    forward(3)
    for p in range(EARLY):
        down_start(p)

    for k in range(4):
        a_local(k).wait()
        a_send(k).wait_recv()
        for j in range(2):
            block = b_buf.at[j, k, other_half]
            pltpu.make_async_copy(block, block, x_rs.at[j, k]).wait()

    def product(r, j, rows):
        total = None
        for k in range(4):
            term = lax.dot_general(
                a_buf[r, k, rows, :],
                b_buf[j, k],
                (((1,), (1,)), ((), ())),
                preferred_element_type=jnp.float32,
            )
            total = term if total is None else total + term
        return total

    def core_copy(r):
        return remote(
            core_send.at[r], core_recv.at[r], c_ss.at[r], c_rs.at[r], dp, hd + 1 - 2 * core
        )

    MM = 256
    for step in range(2):
        r = (1 - y) if step == 0 else y

        @pl.loop(0, row_count // MM)
        def _(i):
            rows = pl.ds(pl.multiple_of(i * MM, MM), MM)
            core_send[r, rows, :] = product(r, 1 - core, rows).astype(jnp.bfloat16)

        core_copy(r).start()

    def y_copy(part_id):
        rows = pl.ds(part_id * MM, MM)
        return remote(
            y_send.at[rows],
            y_recv.at[rows],
            y_ss.at[part_id],
            y_rs.at[part_id],
            dp,
            hd + 2 - 4 * y,
        )

    @pl.loop(0, row_count // MM)
    def _(i):
        rows = pl.ds(pl.multiple_of(i * MM, MM), MM)
        part[rows, :] = product(1 - y, core, rows)

    core_copy(1 - y).wait()
    for piece in range(2):
        rows = pl.ds(piece * MM, MM)
        y_send[rows, :] = (
            part[rows, :] + core_recv[1 - y, rows, :].astype(jnp.float32)
        ).astype(jnp.bfloat16)
        y_copy(piece).start()

    @pl.loop(0, row_count // MM)
    def _(i):
        rows = pl.ds(pl.multiple_of(i * MM, MM), MM)
        part[rows, :] = product(y, core, rows)

    down_forward(0)
    core_copy(y).wait()
    for piece in range(2):
        y_copy(piece).wait()

    @pl.loop(0, row_count // TILE)
    def _(i):
        rows = tile(i)
        total = part[rows, :] + core_recv[y, rows, :].astype(jnp.float32)
        dec[i] = (total + y_recv[rows, :].astype(jnp.float32)).astype(jnp.bfloat16)

    chunk = 2 * (2 * (z // 2) + y) + x
    to_head = 2 * n_group + core

    def slot_copy(i):
        return remote(
            slots_out.at[pl.ds(2 * i, 2)],
            slots_in.at[pl.ds(2 * chunk, 2)],
            s_ss.at[i],
            s_rs.at[chunk],
            i,
            to_head,
        )

    def slot_local(i):
        return pltpu.make_async_copy(
            slots_out.at[pl.ds(2 * i, 2)], slots_in.at[pl.ds(2 * chunk, 2)], s_loc
        )

    def is_me(i):
        return jnp.logical_and(i == dp, to_head == hd)

    @pl.loop(0, 8)
    def _(step):
        i = lax.rem(dp + 1 + step, 8)
        for s in range(2):
            slots_out[2 * i + s] = dec[send_index[(chunk * 8 + i) * 2 + s]]

        @pl.when(is_me(i))
        def _():
            slot_local(i).start()

        @pl.when(jnp.logical_not(is_me(i)))
        def _():
            slot_copy(i).start()

    for p in range(EARLY, n_hid):
        down_start(p)
    down_forward(1)
    down_forward(2)

    @pl.loop(0, 8)
    def _(rho):
        src_z = 2 * (rho // 4) + hd // 2
        src_dp = 2 * src_z + rho % 2
        src_head = 2 * ((rho // 2) % 2) + hd % 2
        own = jnp.logical_and(src_dp == dp, src_head == hd)
        block = slots_in.at[pl.ds(2 * rho, 2)]

        @pl.when(own)
        def _():
            slot_local(dp).wait()

        @pl.when(jnp.logical_not(own))
        def _():
            pltpu.make_async_copy(block, block, s_rs.at[rho]).wait()

    down_forward(3)

    @pl.loop(0, row_count // TILE)
    def _(i):
        rows = tile(i)
        block = slots_in[recv_index[dp * 8 + i]]
        mem[i] = block
        norm_grad = block.astype(jnp.float32) * gain_final
        scaled = out_ref[rows].astype(jnp.float32) * gain_post
        cols[rows] = lanes(row_sum(norm_grad * resid[rows]), row_sum(norm_grad * scaled))

    exchange(2)

    y_head = hd + 2 - 4 * y
    core_head = hd + 1 - 2 * core
    PIECE = 128

    def across_y(piece):
        block = post_buf.at[pl.ds(2 * hd, 2), pl.ds(piece * PIECE, PIECE)]
        return remote(block, block, p_ss.at[0, piece], p_rs.at[0, piece], dp, y_head)

    def across_core(piece):
        block = post_buf.at[pl.ds(2 * hd, 2), pl.ds(piece * PIECE, PIECE)]
        return remote(block, block, p_ss.at[1, piece], p_rs.at[1, piece], dp, core_head)

    def pass_on(piece):
        block = post_buf.at[pl.ds(2 * y_head, 2), pl.ds(piece * PIECE, PIECE)]
        return remote(block, block, q_ss.at[piece], q_rs.at[piece], dp, core_head)

    for piece in range(row_count // PIECE):

        @pl.loop(piece * (PIECE // TILE), (piece + 1) * (PIECE // TILE))
        def _(i):
            rows = tile(i)
            out_scale = out_scale_of(rows)
            resid_scale = resid_scale_of(rows)
            final_mean = resid_scale * stat[2, rows, 0:1] / width
            post_dot = resid_scale * (
                stat[2, rows, 1:2] - resid_scale * final_mean * stat[1, rows, 1:2]
            )
            post_mean = out_scale * post_dot / width
            out_value = out_ref[rows].astype(jnp.float32)
            norm_grad = mem[i].astype(jnp.float32) * gain_final
            total = resid_scale * (norm_grad - resid[rows] * (resid_scale * final_mean))
            resid_grad[rows, :] = total.astype(jnp.bfloat16)
            post_grad = out_scale * (total * gain_post - out_value * (out_scale * post_mean))
            post_half = post_grad.astype(jnp.bfloat16)
            post_buf[2 * hd, rows, :] = post_half[:, : col_share // 2]
            post_buf[2 * hd + 1, rows, :] = post_half[:, col_share // 2 :]

        across_y(piece).start()
        across_core(piece).start()

    down_forward(4)

    for piece in range(row_count // PIECE):
        block = post_buf.at[pl.ds(2 * y_head, 2), pl.ds(piece * PIECE, PIECE)]
        pltpu.make_async_copy(block, block, p_rs.at[0, piece]).wait()
        pass_on(piece).start()
        if piece == 1:
            down_forward(5)

    down_forward(6)

    for piece in range(row_count // PIECE):
        near = post_buf.at[pl.ds(2 * core_head, 2), pl.ds(piece * PIECE, PIECE)]
        pltpu.make_async_copy(near, near, p_rs.at[1, piece]).wait()
        far = post_buf.at[pl.ds(2 * (3 - hd), 2), pl.ds(piece * PIECE, PIECE)]
        pltpu.make_async_copy(far, far, q_rs.at[piece]).wait()

    for p in range(n_hid):
        for src_z in range(4):
            block = down_buf.at[2 * src_z + 1 - x, :, hidden(p)]
            pltpu.make_async_copy(block, block, dx_rs.at[src_z, p]).wait()

        total = None
        for c in range(8):
            term = lax.dot_general(
                post_buf[c],
                down_buf[c, :, hidden(p)],
                (((1,), (0,)), ((), ())),
                preferred_element_type=jnp.float32,
            )
            total = term if total is None else total + term
        acc[...] = total
        for copy in pre_copies(p):
            copy.wait()
        if p >= 2:
            for copy in grad_copies(p - 2):
                copy.wait()

        @pl.loop(0, row_count // TILE)
        def _(i):
            rows = tile(i)
            grad = acc[rows, :]
            value = pre_in[0, p % 2, rows, :].astype(jnp.float32)
            other = pre_in[1, p % 2, rows, :].astype(jnp.float32)
            square = value * value
            bent = jnp.tanh(ROOT * value * (1.0 + CUBIC * square))
            share = 0.5 * (1.0 + bent)
            slope = share + 0.5 * value * (1.0 - bent * bent) * (
                ROOT * (1.0 + 3.0 * CUBIC * square)
            )
            grad_out[0, p % 2, rows, :] = (grad * other * slope).astype(jnp.bfloat16)
            grad_out[1, p % 2, rows, :] = (grad * (value * share)).astype(jnp.bfloat16)

        for copy in grad_copies(p):
            copy.start()
        if p + 2 < n_hid:
            for copy in pre_copies(p + 2):
                copy.start()

    for p in range(n_hid - 2, n_hid):
        for copy in grad_copies(p):
            copy.wait()

    for piece in range(row_count // PIECE):
        across_y(piece).wait_send()
        across_core(piece).wait_send()
        pass_on(piece).wait_send()

    for p in range(n_hid):
        for t in (1, 2, 3):
            down_send(t, p).wait_send()
        for src_z in range(4):
            down_across(src_z, p).wait_send()

    for k in range(4):
        for t in range(2):
            target, copy = b_send(k, t)
            pl.when(target != z)(copy.wait_send)
        a_send(k).wait_send()
        for j in range(2):
            x_send(j, k).wait_send()

    @pl.loop(0, 8)
    def _(i):
        @pl.when(jnp.logical_not(is_me(i)))
        def _():
            slot_copy(i).wait_send()


def block_tables(block_source):
    places = jnp.arange(64, dtype=jnp.int32)
    owner = block_source // 8
    alike = (owner[:, None] == owner[None, :]) & ((places // 8)[:, None] == (places // 8)[None, :])
    before = block_source[None, :] < block_source[:, None]
    rank = jnp.sum((alike & before).astype(jnp.int32), axis=1)
    recv_index = owner * CAP + rank
    slot = (owner * 8 + places // 8) * CAP + rank
    slots = jnp.arange(128, dtype=jnp.int32)
    taken = slot[None, :] == slots[:, None]
    send_index = jnp.sum(jnp.where(taken, (block_source % 8)[None, :], 0), axis=1)
    return send_index, recv_index


def fused_device(
    key_grads,
    value_grads,
    key_weight,
    value_weight,
    block_source,
    hidden_mid,
    mlp_out,
    post_gain,
    final_gain,
    gate_pre,
    up_pre,
    down_weight,
):
    row_count, col_share = hidden_mid.shape
    depth = key_grads.shape[2]
    send_index, recv_index = block_tables(block_source)
    half = jnp.bfloat16
    single = jnp.float32
    dma = pltpu.SemaphoreType.DMA
    anywhere = pl.BlockSpec(memory_space=pl.ANY)
    vmem = pl.BlockSpec(memory_space=pltpu.VMEM)
    smem = pl.BlockSpec(memory_space=pltpu.SMEM)
    n_hid = down_weight.shape[0] // HID
    return pl.pallas_call(
        memory_kernel,
        out_shape=(
            jax.ShapeDtypeStruct((row_count, col_share), half),
            jax.ShapeDtypeStruct(gate_pre.shape, half),
            jax.ShapeDtypeStruct(gate_pre.shape, half),
        ),
        in_specs=[anywhere] * 4 + [smem] * 2 + [vmem] * 4 + [anywhere] * 3,
        out_specs=(vmem, anywhere, anywhere),
        scratch_shapes=[
            pltpu.VMEM((2, 4, row_count, depth), half),
            pltpu.VMEM((2, 4, col_share, depth), half),
            pltpu.VMEM((row_count, col_share), single),
            pltpu.VMEM((2, row_count, col_share), half),
            pltpu.VMEM((2, row_count, col_share), half),
            pltpu.VMEM((row_count, col_share), half),
            pltpu.VMEM((row_count, col_share), half),
            pltpu.VMEM((8, TILE, col_share), half),
            pltpu.VMEM((16, TILE, col_share), half),
            pltpu.VMEM((16, TILE, col_share), half),
            pltpu.VMEM((8, TILE, col_share), half),
            pltpu.VMEM((row_count, col_share), single),
            pltpu.VMEM((row_count, 128), single),
            pltpu.VMEM((128, row_count), single),
            pltpu.VMEM((3, row_count, 128), single),
            pltpu.VMEM((3, 8, row_count), single),
            pltpu.VMEM((3, 3, 8, row_count), single),
            dma((4,)),
            dma((4,)),
            dma((4,)),
            dma((4,)),
            dma((2, 4)),
            dma((2, 4)),
            dma((2, 4)),
            dma((2, 4)),
            dma((2,)),
            dma((2,)),
            dma((2,)),
            dma((2,)),
            dma,
            dma((8,)),
            dma((8,)),
            dma((3, 3)),
            dma((3, 3)),
            dma((2, 4)),
            dma((2, 4)),
            dma((4,)),
            dma((4,)),
            pltpu.VMEM((8, row_count, col_share // 2), half),
            pltpu.VMEM((8,) + down_weight.shape[::-1], half),
            pltpu.VMEM((row_count, HID), single),
            pltpu.VMEM((2, 2, row_count, HID), half),
            pltpu.VMEM((2, 2, row_count, HID), half),
            dma((n_hid,)),
            dma((3, n_hid)),
            dma((4, n_hid)),
            dma((4, n_hid)),
            dma((4, n_hid)),
            dma((2, 2)),
            dma((2, 2)),
        ],
        cost_estimate=pl.CostEstimate(
            flops=100_000_000_000, bytes_accessed=400_000_000, transcendentals=0
        ),
        compiler_params=pltpu.CompilerParams(
            collective_id=0, has_side_effects=True, vmem_limit_bytes=60 * 1024 * 1024
        ),
    )(
        key_grads,
        value_grads,
        key_weight,
        value_weight,
        send_index,
        recv_index,
        hidden_mid,
        mlp_out,
        post_gain[None, :],
        final_gain[None, :],
        down_weight.T,
        gate_pre,
        up_pre,
    )


def solution(mesh):
    return jax.shard_map(
        fused_device if mesh.shape["dp"] == 8 and mesh.shape["head"] == 4 else per_device,
        mesh=mesh,
        in_specs=(
            P(None, "dp", "head"),
            P(None, "dp", "head"),
            P(None, "dp", "head"),
            P(None, "dp", "head"),
            P(),
            P("dp", "head"),
            P("dp", "head"),
            P("head"),
            P("head"),
            P("dp", "head"),
            P("dp", "head"),
            P("head", "dp"),
        ),
        out_specs=(P("dp", "head"), P("dp", "head"), P("dp", "head")),
        check_vma=False,
    )
```

```python
import functools

import jax
import jax.numpy as jnp
from jax import lax
from jax.experimental import pallas as pl
from jax.experimental.pallas import tpu as pltpu
from jax.sharding import PartitionSpec as P

CAP = 2


epsilon = 1e-06


def gelu_parts(gate_value):
    activated, pullback = jax.vjp(
        lambda pre_act: jax.nn.gelu(pre_act, approximate=True), gate_value
    )
    return (activated, pullback(jnp.ones_like(gate_value))[0])


def repack(dec_memory, block_source, dev_blocks):
    row_count, col_share = dec_memory.shape
    block_rows = row_count // dev_blocks
    total_blocks = dev_blocks * dev_blocks
    slot_count = dev_blocks * CAP
    this_dev = lax.axis_index("dp")
    block_ids = jnp.arange(total_blocks, dtype=jnp.int32)
    is_source = block_source[:, None] == block_ids[None, :]
    dest_block = jnp.sum(jnp.where(is_source, block_ids[:, None], 0), axis=0)
    dest_device = (dest_block // dev_blocks).reshape(dev_blocks, dev_blocks)
    same_dest = dest_device[:, :, None] == dest_device[:, None, :]
    slot_ids = jnp.arange(dev_blocks, dtype=jnp.int32)
    before_slot = slot_ids[None, :] < slot_ids[:, None]
    dest_rank = jnp.sum((same_dest & before_slot[None, :, :]).astype(jnp.int32), axis=2)
    own_dest = lax.dynamic_index_in_dim(dest_device, this_dev, 0, keepdims=False)
    own_rank = lax.dynamic_index_in_dim(dest_rank, this_dev, 0, keepdims=False)
    send_slot = own_dest * CAP + own_rank
    buffer_ids = jnp.arange(slot_count, dtype=jnp.int32)
    send_pick = (buffer_ids[:, None] == send_slot[None, :]).astype(jnp.bfloat16)
    local_rows = dec_memory.reshape(dev_blocks, block_rows * col_share)
    outgoing = jnp.dot(send_pick, local_rows, preferred_element_type=jnp.float32).astype(
        jnp.bfloat16
    )
    outgoing = outgoing.reshape(dev_blocks, CAP * block_rows, col_share)
    incoming = lax.all_to_all(outgoing, "dp", split_axis=0, concat_axis=0, tiled=True)
    own_sources = lax.dynamic_slice_in_dim(block_source, this_dev * dev_blocks, dev_blocks)
    source_device = own_sources // dev_blocks
    flat_ranks = dest_rank.reshape(-1)
    source_rank = jnp.sum(
        jnp.where(block_ids[None, :] == own_sources[:, None], flat_ranks[None, :], 0), axis=1
    )
    recv_slot = source_device * CAP + source_rank
    recv_pick = (recv_slot[:, None] == buffer_ids[None, :]).astype(jnp.bfloat16)
    arrived = incoming.reshape(slot_count, block_rows * col_share)
    placed = jnp.dot(recv_pick, arrived, preferred_element_type=jnp.float32).astype(jnp.bfloat16)
    return placed.reshape(row_count, col_share)


def per_device(
    key_grads,
    value_grads,
    key_weight,
    value_weight,
    block_source,
    hidden_mid,
    mlp_out,
    post_gain,
    final_gain,
    gate_pre,
    up_pre,
    down_weight,
):
    row_count, col_share = hidden_mid.shape
    width = col_share * lax.axis_size("head")
    dev_blocks = lax.axis_size("dp")
    key_piece = lax.all_gather(key_weight, "dp", axis=1, tiled=True)
    value_piece = lax.all_gather(value_weight, "dp", axis=1, tiled=True)
    term = jnp.einsum("lrk,lck->rc", key_grads, key_piece, preferred_element_type=jnp.float32)
    term = term + jnp.einsum(
        "lrk,lck->rc", value_grads, value_piece, preferred_element_type=jnp.float32
    )
    dec_memory = lax.psum_scatter(
        term.astype(jnp.bfloat16), "head", scatter_dimension=1, tiled=True
    )
    memory_grad = repack(dec_memory, block_source, dev_blocks)
    mid_value = hidden_mid.astype(jnp.float32)
    out_value = mlp_out.astype(jnp.float32)
    gain_post = post_gain.astype(jnp.float32)
    gain_final = final_gain.astype(jnp.float32)
    sum_out = lax.psum(jnp.sum(out_value * out_value, axis=1), "head")
    out_scale = lax.rsqrt(sum_out / width + epsilon)[:, None]
    resid = mid_value + out_value * out_scale * gain_post
    sum_resid = lax.psum(jnp.sum(resid * resid, axis=1), "head")
    resid_scale = lax.rsqrt(sum_resid / width + epsilon)[:, None]
    norm_grad = memory_grad.astype(jnp.float32) * gain_final
    final_dot = lax.psum(jnp.sum(norm_grad * resid, axis=1), "head")
    final_mean = resid_scale * final_dot[:, None] / width
    resid_total = resid_scale * (norm_grad - resid * resid_scale * final_mean)
    post_input = resid_total * gain_post
    post_dot = lax.psum(jnp.sum(post_input * out_value, axis=1), "head")
    post_mean = out_scale * post_dot[:, None] / width
    post_grad = out_scale * (post_input - out_value * out_scale * post_mean)
    post_full = lax.all_gather(post_grad.astype(jnp.bfloat16), "head", axis=1, tiled=True)
    hidden_grad = lax.dot_general(
        post_full,
        lax.all_gather(down_weight, "dp", axis=1, tiled=True),
        (((1,), (1,)), ((), ())),
        preferred_element_type=jnp.float32,
    )
    activated, slope = gelu_parts(gate_pre.astype(jnp.float32))
    gate_grad = (hidden_grad * up_pre.astype(jnp.float32) * slope).astype(jnp.bfloat16)
    up_grad = (hidden_grad * activated).astype(jnp.bfloat16)
    return (resid_total.astype(jnp.bfloat16), gate_grad, up_grad)


MESH = pl.DeviceIdType.MESH
N_DEV = 32
TILE = 64
HID = 256
EARLY = 3
PLAIN = 4
ROOT = 0.7978845608028654
CUBIC = 0.044715


def remote(src, dst, send_sem, recv_sem, dp_index, head_index):
    return pltpu.make_async_remote_copy(
        src_ref=src,
        dst_ref=dst,
        send_sem=send_sem,
        recv_sem=recv_sem,
        device_id=(dp_index, head_index),
        device_id_type=MESH,
    )


def memory_kernel(
    key_grads,
    value_grads,
    key_weight,
    value_weight,
    send_index,
    recv_index,
    mid_ref,
    out_ref,
    post_ref,
    final_ref,
    down_ref,
    gate_ref,
    up_ref,
    resid_grad,
    gate_grad,
    up_grad,
    a_buf,
    b_buf,
    part,
    core_send,
    core_recv,
    y_send,
    y_recv,
    dec,
    slots_out,
    slots_in,
    mem,
    resid,
    cols,
    rows_buf,
    stat,
    red_out,
    red_in,
    a_loc,
    a_ss,
    a_rs,
    b_loc,
    b_ss,
    b_rs,
    x_ss,
    x_rs,
    c_ss,
    c_rs,
    y_ss,
    y_rs,
    s_loc,
    s_ss,
    s_rs,
    r_ss,
    r_rs,
    p_ss,
    p_rs,
    q_ss,
    q_rs,
    post_buf,
    down_buf,
    acc,
    pre_in,
    grad_out,
    dl_s,
    dz_ss,
    dz_rs,
    dx_ss,
    dx_rs,
    pre_s,
    grad_s,
    pair_buf,
    pair_out,
    pair_in,
    pair_ss,
    pair_rs,
    half_ss,
    half_rs,
):
    row_count, col_share = mid_ref.shape
    width = col_share * 4
    w_rows = key_weight.shape[1]
    dp = lax.axis_index("dp")
    hd = lax.axis_index("head")
    z, x = dp // 2, dp % 2
    y, core = hd // 2, hd % 2
    n_group, z_par = z % 2, z % 2
    me = dp * 4 + hd

    barrier = pltpu.get_barrier_semaphore()

    @pl.loop(0, N_DEV)
    def _(i):
        @pl.when(i != me)
        def _():
            pl.semaphore_signal(barrier, inc=1, device_id=(i // 4, i % 4), device_id_type=MESH)

    pl.semaphore_wait(barrier, N_DEV - 1)

    grads = (key_grads.at[0], key_grads.at[1], value_grads.at[0], value_grads.at[1])
    weights = (key_weight.at[0], key_weight.at[1], value_weight.at[0], value_weight.at[1])
    own_half = pl.ds(pl.multiple_of(x * w_rows, 64), w_rows)
    other_half = pl.ds(pl.multiple_of((1 - x) * w_rows, 64), w_rows)

    def b_send(k, t):
        target = z // 2 + 2 * t
        return target, remote(
            weights[k],
            b_buf.at[z_par, k, own_half],
            b_ss.at[t, k],
            b_rs.at[z_par, k],
            target * 2 + x,
            hd,
        )

    def a_send(k):
        return remote(
            grads[k], a_buf.at[z_par, k], a_ss.at[k], a_rs.at[k], (z + 1 - 2 * z_par) * 2 + x, hd
        )

    def a_local(k):
        return pltpu.make_async_copy(grads[k], a_buf.at[z_par, k], a_loc.at[k])

    def b_local(j, k):
        return pltpu.make_async_copy(weights[k], b_buf.at[j, k, own_half], b_loc.at[k])

    def x_send(j, k):
        block = b_buf.at[j, k, own_half]
        return remote(block, block, x_ss.at[j, k], x_rs.at[j, k], dp + 1 - 2 * x, hd)

    def for_source(j, k, start):
        is_own = 2 * n_group + j == z

        @pl.when(is_own)
        def _():
            if start:
                b_local(j, k).start()
            else:
                b_local(j, k).wait()

        if not start:

            @pl.when(jnp.logical_not(is_own))
            def _():
                block = b_buf.at[j, k, own_half]
                pltpu.make_async_copy(block, block, b_rs.at[j, k]).wait()

    for k in range(4):
        for t in range(2):
            target, copy = b_send(k, t)
            pl.when(target != z)(copy.start)
        for j in range(2):
            for_source(j, k, True)
    for k in range(4):
        a_send(k).start()
        a_local(k).start()

    def forward(k):
        for j in range(2):
            for_source(j, k, False)
            x_send(j, k).start()

    def hidden(p):
        return pl.ds(p * HID, HID)

    def down_local(p):
        return pltpu.make_async_copy(
            down_ref.at[:, hidden(p)], down_buf.at[dp, :, hidden(p)], dl_s.at[p]
        )

    def down_send(t, p):
        return remote(
            down_ref.at[:, hidden(p)],
            down_buf.at[dp, :, hidden(p)],
            dz_ss.at[t - 1, p],
            dz_rs.at[z, p],
            lax.rem(z + t, 4) * 2 + x,
            hd,
        )

    def down_across(src_z, p):
        block = down_buf.at[2 * src_z + x, :, hidden(p)]
        return remote(block, block, dx_ss.at[src_z, p], dx_rs.at[src_z, p], dp + 1 - 2 * x, hd)

    def down_start(p):
        for t in (1, 3, 2):
            down_send(t, p).start()
        down_local(p).wait()
        if p < PLAIN:
            down_across(z, p).start()

    def down_forward(p):
        for t in (1, 3, 2):
            src_z = lax.rem(z + t, 4)
            block = down_buf.at[2 * src_z + x, :, hidden(p)]
            pltpu.make_async_copy(block, block, dz_rs.at[src_z, p]).wait()
            if p < PLAIN:
                down_across(src_z, p).start()

    def pre_copies(p):
        cols_p = hidden(p)
        return (
            pltpu.make_async_copy(gate_ref.at[:, cols_p], pre_in.at[0, p % 2], pre_s.at[0, p % 2]),
            pltpu.make_async_copy(up_ref.at[:, cols_p], pre_in.at[1, p % 2], pre_s.at[1, p % 2]),
        )

    def grad_copies(p):
        cols_p = hidden(p)
        return (
            pltpu.make_async_copy(
                grad_out.at[0, p % 2], gate_grad.at[:, cols_p], grad_s.at[0, p % 2]
            ),
            pltpu.make_async_copy(
                grad_out.at[1, p % 2], up_grad.at[:, cols_p], grad_s.at[1, p % 2]
            ),
        )

    n_hid = down_ref.shape[1] // HID
    for p in range(n_hid):
        down_local(p).start()
    for p in range(2):
        for copy in pre_copies(p):
            copy.start()

    forward(0)

    def exchange(turn):
        rows_t = jnp.transpose(cols[...])
        red_out[turn] = rows_t[0:8]
        copies = []
        for i in range(3):
            copies.append(
                remote(
                    red_out.at[turn],
                    red_in.at[turn, i],
                    r_ss.at[turn, i],
                    r_rs.at[turn, i],
                    dp,
                    lax.rem(hd + 1 + i, 4),
                )
            )
        for copy in copies:
            copy.start()
        for copy in copies:
            copy.wait()
        rows_buf[...] = jnp.zeros_like(rows_buf)
        rows_buf[0:8] = red_out[turn] + red_in[turn, 0] + red_in[turn, 1] + red_in[turn, 2]
        stat[turn] = jnp.transpose(rows_buf[...])

    def lanes(first, second):
        lane = lax.broadcasted_iota(jnp.int32, (TILE, 128), 1)
        return jnp.where(lane == 0, first, jnp.where(lane == 1, second, 0.0))

    def tile(i):
        return pl.ds(pl.multiple_of(i * TILE, TILE), TILE)

    def row_sum(values):
        return jnp.sum(values, axis=1, keepdims=True)

    def out_scale_of(rows):
        return lax.rsqrt(stat[0, rows, 0:1] / width + epsilon)

    def resid_scale_of(rows):
        return lax.rsqrt(stat[1, rows, 0:1] / width + epsilon)

    @pl.loop(0, row_count // TILE)
    def _(i):
        rows = tile(i)
        out_value = out_ref[rows].astype(jnp.float32)
        total = row_sum(out_value * out_value)
        cols[rows] = lanes(total, total)

    exchange(0)
    gain_post = post_ref[...].astype(jnp.float32)
    gain_final = final_ref[...].astype(jnp.float32)

    forward(1)

    @pl.loop(0, row_count // TILE)
    def _(i):
        rows = tile(i)
        scaled = out_ref[rows].astype(jnp.float32) * gain_post
        value = mid_ref[rows].astype(jnp.float32) + scaled * out_scale_of(rows)
        resid[rows] = value
        cols[rows] = lanes(row_sum(value * value), row_sum(value * scaled))

    exchange(1)

    forward(2)
    forward(3)
    for p in range(EARLY):
        down_start(p)

    for k in range(4):
        a_local(k).wait()
        a_send(k).wait_recv()
        for j in range(2):
            block = b_buf.at[j, k, other_half]
            pltpu.make_async_copy(block, block, x_rs.at[j, k]).wait()

    def product(r, j, rows):
        total = None
        for k in range(4):
            term = lax.dot_general(
                a_buf[r, k, rows, :],
                b_buf[j, k],
                (((1,), (1,)), ((), ())),
                preferred_element_type=jnp.float32,
            )
            total = term if total is None else total + term
        return total

    def core_copy(r):
        return remote(
            core_send.at[r], core_recv.at[r], c_ss.at[r], c_rs.at[r], dp, hd + 1 - 2 * core
        )

    MM = 256
    for step in range(2):
        r = (1 - y) if step == 0 else y

        @pl.loop(0, row_count // MM)
        def _(i):
            rows = pl.ds(pl.multiple_of(i * MM, MM), MM)
            core_send[r, rows, :] = product(r, 1 - core, rows).astype(jnp.bfloat16)

        core_copy(r).start()

    def y_copy(part_id):
        rows = pl.ds(part_id * MM, MM)
        return remote(
            y_send.at[rows],
            y_recv.at[rows],
            y_ss.at[part_id],
            y_rs.at[part_id],
            dp,
            hd + 2 - 4 * y,
        )

    @pl.loop(0, row_count // MM)
    def _(i):
        rows = pl.ds(pl.multiple_of(i * MM, MM), MM)
        part[rows, :] = product(1 - y, core, rows)

    core_copy(1 - y).wait()
    for piece in range(2):
        rows = pl.ds(piece * MM, MM)
        y_send[rows, :] = (
            part[rows, :] + core_recv[1 - y, rows, :].astype(jnp.float32)
        ).astype(jnp.bfloat16)
        y_copy(piece).start()

    @pl.loop(0, row_count // MM)
    def _(i):
        rows = pl.ds(pl.multiple_of(i * MM, MM), MM)
        part[rows, :] = product(y, core, rows)

    down_forward(0)
    core_copy(y).wait()
    for piece in range(2):
        y_copy(piece).wait()

    @pl.loop(0, row_count // TILE)
    def _(i):
        rows = tile(i)
        total = part[rows, :] + core_recv[y, rows, :].astype(jnp.float32)
        dec[i] = (total + y_recv[rows, :].astype(jnp.float32)).astype(jnp.bfloat16)

    chunk = 2 * (2 * (z // 2) + y) + x
    to_head = 2 * n_group + core

    def slot_copy(i):
        return remote(
            slots_out.at[pl.ds(2 * i, 2)],
            slots_in.at[pl.ds(2 * chunk, 2)],
            s_ss.at[i],
            s_rs.at[chunk],
            i,
            to_head,
        )

    def slot_local(i):
        return pltpu.make_async_copy(
            slots_out.at[pl.ds(2 * i, 2)], slots_in.at[pl.ds(2 * chunk, 2)], s_loc
        )

    def is_me(i):
        return jnp.logical_and(i == dp, to_head == hd)

    @pl.loop(0, 8)
    def _(step):
        i = lax.rem(dp + 1 + step, 8)
        for s in range(2):
            slots_out[2 * i + s] = dec[send_index[(chunk * 8 + i) * 2 + s]]

        @pl.when(is_me(i))
        def _():
            slot_local(i).start()

        @pl.when(jnp.logical_not(is_me(i)))
        def _():
            slot_copy(i).start()

    for p in range(EARLY, n_hid):
        down_start(p)
    down_forward(1)
    down_forward(2)

    @pl.loop(0, 8)
    def _(rho):
        src_z = 2 * (rho // 4) + hd // 2
        src_dp = 2 * src_z + rho % 2
        src_head = 2 * ((rho // 2) % 2) + hd % 2
        own = jnp.logical_and(src_dp == dp, src_head == hd)
        block = slots_in.at[pl.ds(2 * rho, 2)]

        @pl.when(own)
        def _():
            slot_local(dp).wait()

        @pl.when(jnp.logical_not(own))
        def _():
            pltpu.make_async_copy(block, block, s_rs.at[rho]).wait()

    down_forward(3)

    @pl.loop(0, row_count // TILE)
    def _(i):
        rows = tile(i)
        block = slots_in[recv_index[dp * 8 + i]]
        mem[i] = block
        norm_grad = block.astype(jnp.float32) * gain_final
        scaled = out_ref[rows].astype(jnp.float32) * gain_post
        cols[rows] = lanes(row_sum(norm_grad * resid[rows]), row_sum(norm_grad * scaled))

    exchange(2)

    y_head = hd + 2 - 4 * y
    core_head = hd + 1 - 2 * core
    PIECE = 128

    def across_y(piece):
        block = post_buf.at[pl.ds(2 * hd, 2), pl.ds(piece * PIECE, PIECE)]
        return remote(block, block, p_ss.at[0, piece], p_rs.at[0, piece], dp, y_head)

    def across_core(piece):
        block = post_buf.at[pl.ds(2 * hd, 2), pl.ds(piece * PIECE, PIECE)]
        return remote(block, block, p_ss.at[1, piece], p_rs.at[1, piece], dp, core_head)

    def pass_on(piece):
        block = post_buf.at[pl.ds(2 * y_head, 2), pl.ds(piece * PIECE, PIECE)]
        return remote(block, block, q_ss.at[piece], q_rs.at[piece], dp, core_head)

    for piece in range(row_count // PIECE):

        @pl.loop(piece * (PIECE // TILE), (piece + 1) * (PIECE // TILE))
        def _(i):
            rows = tile(i)
            out_scale = out_scale_of(rows)
            resid_scale = resid_scale_of(rows)
            final_mean = resid_scale * stat[2, rows, 0:1] / width
            post_dot = resid_scale * (
                stat[2, rows, 1:2] - resid_scale * final_mean * stat[1, rows, 1:2]
            )
            post_mean = out_scale * post_dot / width
            out_value = out_ref[rows].astype(jnp.float32)
            norm_grad = mem[i].astype(jnp.float32) * gain_final
            total = resid_scale * (norm_grad - resid[rows] * (resid_scale * final_mean))
            resid_grad[rows, :] = total.astype(jnp.bfloat16)
            post_grad = out_scale * (total * gain_post - out_value * (out_scale * post_mean))
            post_half = post_grad.astype(jnp.bfloat16)
            post_buf[2 * hd, rows, :] = post_half[:, : col_share // 2]
            post_buf[2 * hd + 1, rows, :] = post_half[:, col_share // 2 :]

        across_y(piece).start()
        across_core(piece).start()

    def half_send(i, block, dp_index, head_index):
        return remote(block, block, half_ss.at[i], half_rs.at[i], dp_index, head_index)

    x_half = remote(
        post_buf.at[2 * hd + 1 - x],
        pair_buf.at[hd],
        half_ss.at[0],
        half_rs.at[0],
        dp + 1 - 2 * x,
        hd,
    )
    x_half.start()

    for piece in range(row_count // PIECE):
        block = post_buf.at[pl.ds(2 * y_head, 2), pl.ds(piece * PIECE, PIECE)]
        pltpu.make_async_copy(block, block, p_rs.at[0, piece]).wait()
        pass_on(piece).start()

    x_half.wait_recv()
    y_half = half_send(1, pair_buf.at[hd], dp, y_head)
    core_half = half_send(2, pair_buf.at[hd], dp, core_head)
    y_half.start()
    core_half.start()
    near_half = pair_buf.at[y_head]
    pltpu.make_async_copy(near_half, near_half, half_rs.at[1]).wait()
    far_half = half_send(3, near_half, dp, core_head)
    far_half.start()

    for piece in range(row_count // PIECE):
        near = post_buf.at[pl.ds(2 * core_head, 2), pl.ds(piece * PIECE, PIECE)]
        pltpu.make_async_copy(near, near, p_rs.at[1, piece]).wait()
        far = post_buf.at[pl.ds(2 * (3 - hd), 2), pl.ds(piece * PIECE, PIECE)]
        pltpu.make_async_copy(far, far, q_rs.at[piece]).wait()

    def partial(left, first, count, step, p):
        total = None
        for c in range(count):
            term = lax.dot_general(
                left(c),
                down_buf[first + c * step, :, hidden(p)],
                (((1,), (0,)), ((), ())),
                preferred_element_type=jnp.float32,
            )
            total = term if total is None else total + term
        return total

    def pair_copy(p):
        return remote(
            pair_out.at[p - PLAIN],
            pair_in.at[p - PLAIN],
            pair_ss.at[p - PLAIN],
            pair_rs.at[p - PLAIN],
            dp + 1 - 2 * x,
            hd,
        )

    for p in range(n_hid):
        if p == PLAIN:
            for i, owner in ((2, core_head), (3, 3 - hd)):
                block = pair_buf.at[owner]
                pltpu.make_async_copy(block, block, half_rs.at[i]).wait()
            for later in range(PLAIN, n_hid):
                down_forward(later)
                pair_out[later - PLAIN] = partial(
                    lambda c: pair_buf[c], x, 4, 2, later
                ).astype(jnp.bfloat16)
                pair_copy(later).start()
        if p < PLAIN:
            for src_z in range(4):
                block = down_buf.at[2 * src_z + 1 - x, :, hidden(p)]
                pltpu.make_async_copy(block, block, dx_rs.at[src_z, p]).wait()
            total = partial(lambda c: post_buf[c], 0, 8, 1, p)
        else:
            total = partial(lambda c: post_buf[2 * c + x], x, 4, 2, p)
            pair_copy(p).wait_recv()
            total = total + pair_in[p - PLAIN].astype(jnp.float32)
        acc[...] = total
        for copy in pre_copies(p):
            copy.wait()
        if p >= 2:
            for copy in grad_copies(p - 2):
                copy.wait()

        @pl.loop(0, row_count // TILE)
        def _(i):
            rows = tile(i)
            grad = acc[rows, :]
            value = pre_in[0, p % 2, rows, :].astype(jnp.float32)
            other = pre_in[1, p % 2, rows, :].astype(jnp.float32)
            square = value * value
            bent = jnp.tanh(ROOT * value * (1.0 + CUBIC * square))
            share = 0.5 * (1.0 + bent)
            slope = share + 0.5 * value * (1.0 - bent * bent) * (
                ROOT * (1.0 + 3.0 * CUBIC * square)
            )
            grad_out[0, p % 2, rows, :] = (grad * other * slope).astype(jnp.bfloat16)
            grad_out[1, p % 2, rows, :] = (grad * (value * share)).astype(jnp.bfloat16)

        for copy in grad_copies(p):
            copy.start()
        if p + 2 < n_hid:
            for copy in pre_copies(p + 2):
                copy.start()

    for p in range(n_hid - 2, n_hid):
        for copy in grad_copies(p):
            copy.wait()

    for piece in range(row_count // PIECE):
        across_y(piece).wait_send()
        across_core(piece).wait_send()
        pass_on(piece).wait_send()

    for p in range(n_hid):
        for t in (1, 2, 3):
            down_send(t, p).wait_send()
        if p < PLAIN:
            for src_z in range(4):
                down_across(src_z, p).wait_send()
        else:
            pair_copy(p).wait_send()
    for copy in (x_half, y_half, core_half, far_half):
        copy.wait_send()

    for k in range(4):
        for t in range(2):
            target, copy = b_send(k, t)
            pl.when(target != z)(copy.wait_send)
        a_send(k).wait_send()
        for j in range(2):
            x_send(j, k).wait_send()

    @pl.loop(0, 8)
    def _(i):
        @pl.when(jnp.logical_not(is_me(i)))
        def _():
            slot_copy(i).wait_send()


def block_tables(block_source):
    places = jnp.arange(64, dtype=jnp.int32)
    owner = block_source // 8
    alike = (owner[:, None] == owner[None, :]) & ((places // 8)[:, None] == (places // 8)[None, :])
    before = block_source[None, :] < block_source[:, None]
    rank = jnp.sum((alike & before).astype(jnp.int32), axis=1)
    recv_index = owner * CAP + rank
    slot = (owner * 8 + places // 8) * CAP + rank
    slots = jnp.arange(128, dtype=jnp.int32)
    taken = slot[None, :] == slots[:, None]
    send_index = jnp.sum(jnp.where(taken, (block_source % 8)[None, :], 0), axis=1)
    return send_index, recv_index


def fused_device(
    key_grads,
    value_grads,
    key_weight,
    value_weight,
    block_source,
    hidden_mid,
    mlp_out,
    post_gain,
    final_gain,
    gate_pre,
    up_pre,
    down_weight,
):
    row_count, col_share = hidden_mid.shape
    depth = key_grads.shape[2]
    send_index, recv_index = block_tables(block_source)
    half = jnp.bfloat16
    single = jnp.float32
    dma = pltpu.SemaphoreType.DMA
    anywhere = pl.BlockSpec(memory_space=pl.ANY)
    vmem = pl.BlockSpec(memory_space=pltpu.VMEM)
    smem = pl.BlockSpec(memory_space=pltpu.SMEM)
    n_hid = down_weight.shape[0] // HID
    return pl.pallas_call(
        memory_kernel,
        out_shape=(
            jax.ShapeDtypeStruct((row_count, col_share), half),
            jax.ShapeDtypeStruct(gate_pre.shape, half),
            jax.ShapeDtypeStruct(gate_pre.shape, half),
        ),
        in_specs=[anywhere] * 4 + [smem] * 2 + [vmem] * 4 + [anywhere] * 3,
        out_specs=(vmem, anywhere, anywhere),
        scratch_shapes=[
            pltpu.VMEM((2, 4, row_count, depth), half),
            pltpu.VMEM((2, 4, col_share, depth), half),
            pltpu.VMEM((row_count, col_share), single),
            pltpu.VMEM((2, row_count, col_share), half),
            pltpu.VMEM((2, row_count, col_share), half),
            pltpu.VMEM((row_count, col_share), half),
            pltpu.VMEM((row_count, col_share), half),
            pltpu.VMEM((8, TILE, col_share), half),
            pltpu.VMEM((16, TILE, col_share), half),
            pltpu.VMEM((16, TILE, col_share), half),
            pltpu.VMEM((8, TILE, col_share), half),
            pltpu.VMEM((row_count, col_share), single),
            pltpu.VMEM((row_count, 128), single),
            pltpu.VMEM((128, row_count), single),
            pltpu.VMEM((3, row_count, 128), single),
            pltpu.VMEM((3, 8, row_count), single),
            pltpu.VMEM((3, 3, 8, row_count), single),
            dma((4,)),
            dma((4,)),
            dma((4,)),
            dma((4,)),
            dma((2, 4)),
            dma((2, 4)),
            dma((2, 4)),
            dma((2, 4)),
            dma((2,)),
            dma((2,)),
            dma((2,)),
            dma((2,)),
            dma,
            dma((8,)),
            dma((8,)),
            dma((3, 3)),
            dma((3, 3)),
            dma((2, 4)),
            dma((2, 4)),
            dma((4,)),
            dma((4,)),
            pltpu.VMEM((8, row_count, col_share // 2), half),
            pltpu.VMEM((8,) + down_weight.shape[::-1], half),
            pltpu.VMEM((row_count, HID), single),
            pltpu.VMEM((2, 2, row_count, HID), half),
            pltpu.VMEM((2, 2, row_count, HID), half),
            dma((n_hid,)),
            dma((3, n_hid)),
            dma((4, n_hid)),
            dma((4, n_hid)),
            dma((4, n_hid)),
            dma((2, 2)),
            dma((2, 2)),
            pltpu.VMEM((4, row_count, col_share // 2), half),
            pltpu.VMEM((n_hid - PLAIN, row_count, HID), half),
            pltpu.VMEM((n_hid - PLAIN, row_count, HID), half),
            dma((n_hid - PLAIN,)),
            dma((n_hid - PLAIN,)),
            dma((4,)),
            dma((4,)),
        ],
        cost_estimate=pl.CostEstimate(
            flops=100_000_000_000, bytes_accessed=400_000_000, transcendentals=0
        ),
        compiler_params=pltpu.CompilerParams(
            collective_id=0, has_side_effects=True, vmem_limit_bytes=60 * 1024 * 1024
        ),
    )(
        key_grads,
        value_grads,
        key_weight,
        value_weight,
        send_index,
        recv_index,
        hidden_mid,
        mlp_out,
        post_gain[None, :],
        final_gain[None, :],
        down_weight.T,
        gate_pre,
        up_pre,
    )


def solution(mesh):
    return jax.shard_map(
        fused_device if mesh.shape["dp"] == 8 and mesh.shape["head"] == 4 else per_device,
        mesh=mesh,
        in_specs=(
            P(None, "dp", "head"),
            P(None, "dp", "head"),
            P(None, "dp", "head"),
            P(None, "dp", "head"),
            P(),
            P("dp", "head"),
            P("dp", "head"),
            P("head"),
            P("head"),
            P("dp", "head"),
            P("dp", "head"),
            P("head", "dp"),
        ),
        out_specs=(P("dp", "head"), P("dp", "head"), P("dp", "head")),
        check_vma=False,
    )
```

```python
import functools

import jax
import jax.numpy as jnp
from jax import lax
from jax.experimental import pallas as pl
from jax.experimental.pallas import tpu as pltpu
from jax.sharding import PartitionSpec as P

CAP = 2


epsilon = 1e-06


def gelu_parts(gate_value):
    activated, pullback = jax.vjp(
        lambda pre_act: jax.nn.gelu(pre_act, approximate=True), gate_value
    )
    return (activated, pullback(jnp.ones_like(gate_value))[0])


def repack(dec_memory, block_source, dev_blocks):
    row_count, col_share = dec_memory.shape
    block_rows = row_count // dev_blocks
    total_blocks = dev_blocks * dev_blocks
    slot_count = dev_blocks * CAP
    this_dev = lax.axis_index("dp")
    block_ids = jnp.arange(total_blocks, dtype=jnp.int32)
    is_source = block_source[:, None] == block_ids[None, :]
    dest_block = jnp.sum(jnp.where(is_source, block_ids[:, None], 0), axis=0)
    dest_device = (dest_block // dev_blocks).reshape(dev_blocks, dev_blocks)
    same_dest = dest_device[:, :, None] == dest_device[:, None, :]
    slot_ids = jnp.arange(dev_blocks, dtype=jnp.int32)
    before_slot = slot_ids[None, :] < slot_ids[:, None]
    dest_rank = jnp.sum((same_dest & before_slot[None, :, :]).astype(jnp.int32), axis=2)
    own_dest = lax.dynamic_index_in_dim(dest_device, this_dev, 0, keepdims=False)
    own_rank = lax.dynamic_index_in_dim(dest_rank, this_dev, 0, keepdims=False)
    send_slot = own_dest * CAP + own_rank
    buffer_ids = jnp.arange(slot_count, dtype=jnp.int32)
    send_pick = (buffer_ids[:, None] == send_slot[None, :]).astype(jnp.bfloat16)
    local_rows = dec_memory.reshape(dev_blocks, block_rows * col_share)
    outgoing = jnp.dot(send_pick, local_rows, preferred_element_type=jnp.float32).astype(
        jnp.bfloat16
    )
    outgoing = outgoing.reshape(dev_blocks, CAP * block_rows, col_share)
    incoming = lax.all_to_all(outgoing, "dp", split_axis=0, concat_axis=0, tiled=True)
    own_sources = lax.dynamic_slice_in_dim(block_source, this_dev * dev_blocks, dev_blocks)
    source_device = own_sources // dev_blocks
    flat_ranks = dest_rank.reshape(-1)
    source_rank = jnp.sum(
        jnp.where(block_ids[None, :] == own_sources[:, None], flat_ranks[None, :], 0), axis=1
    )
    recv_slot = source_device * CAP + source_rank
    recv_pick = (recv_slot[:, None] == buffer_ids[None, :]).astype(jnp.bfloat16)
    arrived = incoming.reshape(slot_count, block_rows * col_share)
    placed = jnp.dot(recv_pick, arrived, preferred_element_type=jnp.float32).astype(jnp.bfloat16)
    return placed.reshape(row_count, col_share)


def per_device(
    key_grads,
    value_grads,
    key_weight,
    value_weight,
    block_source,
    hidden_mid,
    mlp_out,
    post_gain,
    final_gain,
    gate_pre,
    up_pre,
    down_weight,
):
    row_count, col_share = hidden_mid.shape
    width = col_share * lax.axis_size("head")
    dev_blocks = lax.axis_size("dp")
    key_piece = lax.all_gather(key_weight, "dp", axis=1, tiled=True)
    value_piece = lax.all_gather(value_weight, "dp", axis=1, tiled=True)
    term = jnp.einsum("lrk,lck->rc", key_grads, key_piece, preferred_element_type=jnp.float32)
    term = term + jnp.einsum(
        "lrk,lck->rc", value_grads, value_piece, preferred_element_type=jnp.float32
    )
    dec_memory = lax.psum_scatter(
        term.astype(jnp.bfloat16), "head", scatter_dimension=1, tiled=True
    )
    memory_grad = repack(dec_memory, block_source, dev_blocks)
    mid_value = hidden_mid.astype(jnp.float32)
    out_value = mlp_out.astype(jnp.float32)
    gain_post = post_gain.astype(jnp.float32)
    gain_final = final_gain.astype(jnp.float32)
    sum_out = lax.psum(jnp.sum(out_value * out_value, axis=1), "head")
    out_scale = lax.rsqrt(sum_out / width + epsilon)[:, None]
    resid = mid_value + out_value * out_scale * gain_post
    sum_resid = lax.psum(jnp.sum(resid * resid, axis=1), "head")
    resid_scale = lax.rsqrt(sum_resid / width + epsilon)[:, None]
    norm_grad = memory_grad.astype(jnp.float32) * gain_final
    final_dot = lax.psum(jnp.sum(norm_grad * resid, axis=1), "head")
    final_mean = resid_scale * final_dot[:, None] / width
    resid_total = resid_scale * (norm_grad - resid * resid_scale * final_mean)
    post_input = resid_total * gain_post
    post_dot = lax.psum(jnp.sum(post_input * out_value, axis=1), "head")
    post_mean = out_scale * post_dot[:, None] / width
    post_grad = out_scale * (post_input - out_value * out_scale * post_mean)
    post_full = lax.all_gather(post_grad.astype(jnp.bfloat16), "head", axis=1, tiled=True)
    hidden_grad = lax.dot_general(
        post_full,
        lax.all_gather(down_weight, "dp", axis=1, tiled=True),
        (((1,), (1,)), ((), ())),
        preferred_element_type=jnp.float32,
    )
    activated, slope = gelu_parts(gate_pre.astype(jnp.float32))
    gate_grad = (hidden_grad * up_pre.astype(jnp.float32) * slope).astype(jnp.bfloat16)
    up_grad = (hidden_grad * activated).astype(jnp.bfloat16)
    return (resid_total.astype(jnp.bfloat16), gate_grad, up_grad)


MESH = pl.DeviceIdType.MESH
N_DEV = 32
TILE = 64
HID = 256
EARLY = 3
ROOT = 0.7978845608028654
CUBIC = 0.044715


def remote(src, dst, send_sem, recv_sem, dp_index, head_index):
    return pltpu.make_async_remote_copy(
        src_ref=src,
        dst_ref=dst,
        send_sem=send_sem,
        recv_sem=recv_sem,
        device_id=(dp_index, head_index),
        device_id_type=MESH,
    )


def memory_kernel(
    key_grads,
    value_grads,
    key_weight,
    value_weight,
    send_index,
    recv_index,
    mid_ref,
    out_ref,
    post_ref,
    final_ref,
    down_ref,
    gate_ref,
    up_ref,
    resid_grad,
    gate_grad,
    up_grad,
    a_buf,
    b_buf,
    part,
    core_send,
    core_recv,
    y_send,
    y_recv,
    dec,
    slots_out,
    slots_in,
    mem,
    resid,
    cols,
    rows_buf,
    stat,
    red_out,
    red_in,
    a_loc,
    a_ss,
    a_rs,
    b_loc,
    b_ss,
    b_rs,
    x_ss,
    x_rs,
    c_ss,
    c_rs,
    y_ss,
    y_rs,
    s_loc,
    s_ss,
    s_rs,
    r_ss,
    r_rs,
    p_ss,
    p_rs,
    q_ss,
    q_rs,
    post_buf,
    down_buf,
    acc,
    pre_in,
    grad_out,
    dl_s,
    dz_ss,
    dz_rs,
    dx_ss,
    dx_rs,
    pre_s,
    grad_s,
):
    row_count, col_share = mid_ref.shape
    width = col_share * 4
    w_rows = key_weight.shape[1]
    dp = lax.axis_index("dp")
    hd = lax.axis_index("head")
    z, x = dp // 2, dp % 2
    y, core = hd // 2, hd % 2
    n_group, z_par = z % 2, z % 2
    me = dp * 4 + hd

    barrier = pltpu.get_barrier_semaphore()

    @pl.loop(0, N_DEV)
    def _(i):
        @pl.when(i != me)
        def _():
            pl.semaphore_signal(barrier, inc=1, device_id=(i // 4, i % 4), device_id_type=MESH)

    pl.semaphore_wait(barrier, N_DEV - 1)

    grads = (key_grads.at[0], key_grads.at[1], value_grads.at[0], value_grads.at[1])
    weights = (key_weight.at[0], key_weight.at[1], value_weight.at[0], value_weight.at[1])
    own_half = pl.ds(pl.multiple_of(x * w_rows, 64), w_rows)
    other_half = pl.ds(pl.multiple_of((1 - x) * w_rows, 64), w_rows)

    def b_send(k, t):
        target = z // 2 + 2 * t
        return target, remote(
            weights[k],
            b_buf.at[z_par, k, own_half],
            b_ss.at[t, k],
            b_rs.at[z_par, k],
            target * 2 + x,
            hd,
        )

    def a_send(k):
        return remote(
            grads[k], a_buf.at[z_par, k], a_ss.at[k], a_rs.at[k], (z + 1 - 2 * z_par) * 2 + x, hd
        )

    def a_local(k):
        return pltpu.make_async_copy(grads[k], a_buf.at[z_par, k], a_loc.at[k])

    def b_local(j, k):
        return pltpu.make_async_copy(weights[k], b_buf.at[j, k, own_half], b_loc.at[k])

    def x_send(j, k):
        block = b_buf.at[j, k, own_half]
        return remote(block, block, x_ss.at[j, k], x_rs.at[j, k], dp + 1 - 2 * x, hd)

    def for_source(j, k, start):
        is_own = 2 * n_group + j == z

        @pl.when(is_own)
        def _():
            if start:
                b_local(j, k).start()
            else:
                b_local(j, k).wait()

        if not start:

            @pl.when(jnp.logical_not(is_own))
            def _():
                block = b_buf.at[j, k, own_half]
                pltpu.make_async_copy(block, block, b_rs.at[j, k]).wait()

    for k in range(4):
        for t in range(2):
            target, copy = b_send(k, t)
            pl.when(target != z)(copy.start)
        for j in range(2):
            for_source(j, k, True)
    for k in range(4):
        a_send(k).start()
        a_local(k).start()

    def forward(k):
        for j in range(2):
            for_source(j, k, False)
            x_send(j, k).start()

    def hidden(p):
        return pl.ds(p * HID, HID)

    def down_local(p):
        return pltpu.make_async_copy(
            down_ref.at[:, hidden(p)], down_buf.at[dp, :, hidden(p)], dl_s.at[p]
        )

    def down_send(t, p):
        return remote(
            down_ref.at[:, hidden(p)],
            down_buf.at[dp, :, hidden(p)],
            dz_ss.at[t - 1, p],
            dz_rs.at[z, p],
            lax.rem(z + t, 4) * 2 + x,
            hd,
        )

    def down_across(src_z, p):
        block = down_buf.at[2 * src_z + x, :, hidden(p)]
        return remote(block, block, dx_ss.at[src_z, p], dx_rs.at[src_z, p], dp + 1 - 2 * x, hd)

    def down_start(p):
        for t in (1, 3, 2):
            down_send(t, p).start()
        down_local(p).wait()
        down_across(z, p).start()

    def down_forward(p):
        for t in (1, 3, 2):
            src_z = lax.rem(z + t, 4)
            block = down_buf.at[2 * src_z + x, :, hidden(p)]
            pltpu.make_async_copy(block, block, dz_rs.at[src_z, p]).wait()
            down_across(src_z, p).start()

    def pre_copies(p):
        cols_p = hidden(p)
        return (
            pltpu.make_async_copy(gate_ref.at[:, cols_p], pre_in.at[0, p % 2], pre_s.at[0, p % 2]),
            pltpu.make_async_copy(up_ref.at[:, cols_p], pre_in.at[1, p % 2], pre_s.at[1, p % 2]),
        )

    def grad_copies(p):
        cols_p = hidden(p)
        return (
            pltpu.make_async_copy(
                grad_out.at[0, p % 2], gate_grad.at[:, cols_p], grad_s.at[0, p % 2]
            ),
            pltpu.make_async_copy(
                grad_out.at[1, p % 2], up_grad.at[:, cols_p], grad_s.at[1, p % 2]
            ),
        )

    n_hid = down_ref.shape[1] // HID
    for p in range(n_hid):
        down_local(p).start()
    for p in range(2):
        for copy in pre_copies(p):
            copy.start()

    forward(0)

    def exchange(turn):
        rows_t = jnp.transpose(cols[...])
        red_out[turn] = rows_t[0:8]
        copies = []
        for i in range(3):
            copies.append(
                remote(
                    red_out.at[turn],
                    red_in.at[turn, i],
                    r_ss.at[turn, i],
                    r_rs.at[turn, i],
                    dp,
                    lax.rem(hd + 1 + i, 4),
                )
            )
        for copy in copies:
            copy.start()
        for copy in copies:
            copy.wait()
        rows_buf[...] = jnp.zeros_like(rows_buf)
        rows_buf[0:8] = red_out[turn] + red_in[turn, 0] + red_in[turn, 1] + red_in[turn, 2]
        stat[turn] = jnp.transpose(rows_buf[...])

    def lanes(first, second):
        lane = lax.broadcasted_iota(jnp.int32, (TILE, 128), 1)
        return jnp.where(lane == 0, first, jnp.where(lane == 1, second, 0.0))

    def tile(i):
        return pl.ds(pl.multiple_of(i * TILE, TILE), TILE)

    def row_sum(values):
        return jnp.sum(values, axis=1, keepdims=True)

    def out_scale_of(rows):
        return lax.rsqrt(stat[0, rows, 0:1] / width + epsilon)

    def resid_scale_of(rows):
        return lax.rsqrt(stat[1, rows, 0:1] / width + epsilon)

    @pl.loop(0, row_count // TILE)
    def _(i):
        rows = tile(i)
        out_value = out_ref[rows].astype(jnp.float32)
        total = row_sum(out_value * out_value)
        cols[rows] = lanes(total, total)

    exchange(0)
    gain_post = post_ref[...].astype(jnp.float32)
    gain_final = final_ref[...].astype(jnp.float32)

    forward(1)

    @pl.loop(0, row_count // TILE)
    def _(i):
        rows = tile(i)
        scaled = out_ref[rows].astype(jnp.float32) * gain_post
        value = mid_ref[rows].astype(jnp.float32) + scaled * out_scale_of(rows)
        resid[rows] = value
        cols[rows] = lanes(row_sum(value * value), row_sum(value * scaled))

    exchange(1)

    forward(2)
    forward(3)
    for p in range(EARLY):
        down_start(p)

    for k in range(4):
        a_local(k).wait()
        a_send(k).wait_recv()
        for j in range(2):
            block = b_buf.at[j, k, other_half]
            pltpu.make_async_copy(block, block, x_rs.at[j, k]).wait()

    def product(r, j, rows):
        total = None
        for k in range(4):
            term = lax.dot_general(
                a_buf[r, k, rows, :],
                b_buf[j, k],
                (((1,), (1,)), ((), ())),
                preferred_element_type=jnp.float32,
            )
            total = term if total is None else total + term
        return total

    def core_copy(r):
        return remote(
            core_send.at[r], core_recv.at[r], c_ss.at[r], c_rs.at[r], dp, hd + 1 - 2 * core
        )

    MM = 256
    for step in range(2):
        r = (1 - y) if step == 0 else y

        @pl.loop(0, row_count // MM)
        def _(i):
            rows = pl.ds(pl.multiple_of(i * MM, MM), MM)
            core_send[r, rows, :] = product(r, 1 - core, rows).astype(jnp.bfloat16)

        core_copy(r).start()

    def y_copy(part_id):
        rows = pl.ds(part_id * MM, MM)
        return remote(
            y_send.at[rows],
            y_recv.at[rows],
            y_ss.at[part_id],
            y_rs.at[part_id],
            dp,
            hd + 2 - 4 * y,
        )

    @pl.loop(0, row_count // MM)
    def _(i):
        rows = pl.ds(pl.multiple_of(i * MM, MM), MM)
        part[rows, :] = product(1 - y, core, rows)

    core_copy(1 - y).wait()
    for piece in range(2):
        rows = pl.ds(piece * MM, MM)
        y_send[rows, :] = (
            part[rows, :] + core_recv[1 - y, rows, :].astype(jnp.float32)
        ).astype(jnp.bfloat16)
        y_copy(piece).start()

    @pl.loop(0, row_count // MM)
    def _(i):
        rows = pl.ds(pl.multiple_of(i * MM, MM), MM)
        part[rows, :] = product(y, core, rows)

    down_forward(0)
    core_copy(y).wait()
    for piece in range(2):
        y_copy(piece).wait()

    @pl.loop(0, row_count // TILE)
    def _(i):
        rows = tile(i)
        total = part[rows, :] + core_recv[y, rows, :].astype(jnp.float32)
        dec[i] = (total + y_recv[rows, :].astype(jnp.float32)).astype(jnp.bfloat16)

    chunk = 2 * (2 * (z // 2) + y) + x
    to_head = 2 * n_group + core

    def slot_copy(i):
        return remote(
            slots_out.at[pl.ds(2 * i, 2)],
            slots_in.at[pl.ds(2 * chunk, 2)],
            s_ss.at[i],
            s_rs.at[chunk],
            i,
            to_head,
        )

    def slot_local(i):
        return pltpu.make_async_copy(
            slots_out.at[pl.ds(2 * i, 2)], slots_in.at[pl.ds(2 * chunk, 2)], s_loc
        )

    def is_me(i):
        return jnp.logical_and(i == dp, to_head == hd)

    @pl.loop(0, 8)
    def _(step):
        i = lax.rem(dp + 1 + step, 8)
        for s in range(2):
            slots_out[2 * i + s] = dec[send_index[(chunk * 8 + i) * 2 + s]]

        @pl.when(is_me(i))
        def _():
            slot_local(i).start()

        @pl.when(jnp.logical_not(is_me(i)))
        def _():
            slot_copy(i).start()

    for p in range(EARLY, n_hid):
        down_start(p)
    down_forward(1)
    down_forward(2)

    @pl.loop(0, 8)
    def _(rho):
        src_z = 2 * (rho // 4) + hd // 2
        src_dp = 2 * src_z + rho % 2
        src_head = 2 * ((rho // 2) % 2) + hd % 2
        own = jnp.logical_and(src_dp == dp, src_head == hd)
        block = slots_in.at[pl.ds(2 * rho, 2)]

        @pl.when(own)
        def _():
            slot_local(dp).wait()

        @pl.when(jnp.logical_not(own))
        def _():
            pltpu.make_async_copy(block, block, s_rs.at[rho]).wait()

    @pl.loop(0, row_count // TILE)
    def _(i):
        rows = tile(i)
        block = slots_in[recv_index[dp * 8 + i]]
        mem[i] = block
        norm_grad = block.astype(jnp.float32) * gain_final
        scaled = out_ref[rows].astype(jnp.float32) * gain_post
        cols[rows] = lanes(row_sum(norm_grad * resid[rows]), row_sum(norm_grad * scaled))

    exchange(2)

    y_head = hd + 2 - 4 * y
    core_head = hd + 1 - 2 * core
    PIECE = 128

    def across_y(piece):
        block = post_buf.at[pl.ds(2 * hd, 2), pl.ds(piece * PIECE, PIECE)]
        return remote(block, block, p_ss.at[0, piece], p_rs.at[0, piece], dp, y_head)

    def across_core(piece):
        block = post_buf.at[pl.ds(2 * hd, 2), pl.ds(piece * PIECE, PIECE)]
        return remote(block, block, p_ss.at[1, piece], p_rs.at[1, piece], dp, core_head)

    def pass_on(piece):
        block = post_buf.at[pl.ds(2 * y_head, 2), pl.ds(piece * PIECE, PIECE)]
        return remote(block, block, q_ss.at[piece], q_rs.at[piece], dp, core_head)

    for piece in range(row_count // PIECE):

        @pl.loop(piece * (PIECE // TILE), (piece + 1) * (PIECE // TILE))
        def _(i):
            rows = tile(i)
            out_scale = out_scale_of(rows)
            resid_scale = resid_scale_of(rows)
            final_mean = resid_scale * stat[2, rows, 0:1] / width
            post_dot = resid_scale * (
                stat[2, rows, 1:2] - resid_scale * final_mean * stat[1, rows, 1:2]
            )
            post_mean = out_scale * post_dot / width
            out_value = out_ref[rows].astype(jnp.float32)
            norm_grad = mem[i].astype(jnp.float32) * gain_final
            total = resid_scale * (norm_grad - resid[rows] * (resid_scale * final_mean))
            resid_grad[rows, :] = total.astype(jnp.bfloat16)
            post_grad = out_scale * (total * gain_post - out_value * (out_scale * post_mean))
            post_half = post_grad.astype(jnp.bfloat16)
            post_buf[2 * hd, rows, :] = post_half[:, : col_share // 2]
            post_buf[2 * hd + 1, rows, :] = post_half[:, col_share // 2 :]

        across_y(piece).start()
        across_core(piece).start()

    down_forward(3)

    for piece in range(row_count // PIECE):
        block = post_buf.at[pl.ds(2 * y_head, 2), pl.ds(piece * PIECE, PIECE)]
        pltpu.make_async_copy(block, block, p_rs.at[0, piece]).wait()
        pass_on(piece).start()

    for p in range(EARLY + 1, n_hid):
        down_forward(p)

    for piece in range(row_count // PIECE):
        near = post_buf.at[pl.ds(2 * core_head, 2), pl.ds(piece * PIECE, PIECE)]
        pltpu.make_async_copy(near, near, p_rs.at[1, piece]).wait()
        far = post_buf.at[pl.ds(2 * (3 - hd), 2), pl.ds(piece * PIECE, PIECE)]
        pltpu.make_async_copy(far, far, q_rs.at[piece]).wait()

    for p in range(n_hid):
        for src_z in range(4):
            block = down_buf.at[2 * src_z + 1 - x, :, hidden(p)]
            pltpu.make_async_copy(block, block, dx_rs.at[src_z, p]).wait()

        total = None
        for c in range(8):
            term = lax.dot_general(
                post_buf[c],
                down_buf[c, :, hidden(p)],
                (((1,), (0,)), ((), ())),
                preferred_element_type=jnp.float32,
            )
            total = term if total is None else total + term
        acc[...] = total
        for copy in pre_copies(p):
            copy.wait()
        if p >= 2:
            for copy in grad_copies(p - 2):
                copy.wait()

        @pl.loop(0, row_count // TILE)
        def _(i):
            rows = tile(i)
            grad = acc[rows, :]
            value = pre_in[0, p % 2, rows, :].astype(jnp.float32)
            other = pre_in[1, p % 2, rows, :].astype(jnp.float32)
            square = value * value
            bent = jnp.tanh(ROOT * value * (1.0 + CUBIC * square))
            share = 0.5 * (1.0 + bent)
            slope = share + 0.5 * value * (1.0 - bent * bent) * (
                ROOT * (1.0 + 3.0 * CUBIC * square)
            )
            grad_out[0, p % 2, rows, :] = (grad * other * slope).astype(jnp.bfloat16)
            grad_out[1, p % 2, rows, :] = (grad * (value * share)).astype(jnp.bfloat16)

        for copy in grad_copies(p):
            copy.start()
        if p + 2 < n_hid:
            for copy in pre_copies(p + 2):
                copy.start()

    for p in range(n_hid - 2, n_hid):
        for copy in grad_copies(p):
            copy.wait()

    for piece in range(row_count // PIECE):
        across_y(piece).wait_send()
        across_core(piece).wait_send()
        pass_on(piece).wait_send()

    for p in range(n_hid):
        for t in (1, 2, 3):
            down_send(t, p).wait_send()
        for src_z in range(4):
            down_across(src_z, p).wait_send()

    for k in range(4):
        for t in range(2):
            target, copy = b_send(k, t)
            pl.when(target != z)(copy.wait_send)
        a_send(k).wait_send()
        for j in range(2):
            x_send(j, k).wait_send()

    @pl.loop(0, 8)
    def _(i):
        @pl.when(jnp.logical_not(is_me(i)))
        def _():
            slot_copy(i).wait_send()


def block_tables(block_source):
    places = jnp.arange(64, dtype=jnp.int32)
    owner = block_source // 8
    alike = (owner[:, None] == owner[None, :]) & ((places // 8)[:, None] == (places // 8)[None, :])
    before = block_source[None, :] < block_source[:, None]
    rank = jnp.sum((alike & before).astype(jnp.int32), axis=1)
    recv_index = owner * CAP + rank
    slot = (owner * 8 + places // 8) * CAP + rank
    slots = jnp.arange(128, dtype=jnp.int32)
    taken = slot[None, :] == slots[:, None]
    send_index = jnp.sum(jnp.where(taken, (block_source % 8)[None, :], 0), axis=1)
    return send_index, recv_index


def fused_device(
    key_grads,
    value_grads,
    key_weight,
    value_weight,
    block_source,
    hidden_mid,
    mlp_out,
    post_gain,
    final_gain,
    gate_pre,
    up_pre,
    down_weight,
):
    row_count, col_share = hidden_mid.shape
    depth = key_grads.shape[2]
    send_index, recv_index = block_tables(block_source)
    half = jnp.bfloat16
    single = jnp.float32
    dma = pltpu.SemaphoreType.DMA
    anywhere = pl.BlockSpec(memory_space=pl.ANY)
    vmem = pl.BlockSpec(memory_space=pltpu.VMEM)
    smem = pl.BlockSpec(memory_space=pltpu.SMEM)
    n_hid = down_weight.shape[0] // HID
    return pl.pallas_call(
        memory_kernel,
        out_shape=(
            jax.ShapeDtypeStruct((row_count, col_share), half),
            jax.ShapeDtypeStruct(gate_pre.shape, half),
            jax.ShapeDtypeStruct(gate_pre.shape, half),
        ),
        in_specs=[anywhere] * 4 + [smem] * 2 + [vmem] * 4 + [anywhere] * 3,
        out_specs=(vmem, anywhere, anywhere),
        scratch_shapes=[
            pltpu.VMEM((2, 4, row_count, depth), half),
            pltpu.VMEM((2, 4, col_share, depth), half),
            pltpu.VMEM((row_count, col_share), single),
            pltpu.VMEM((2, row_count, col_share), half),
            pltpu.VMEM((2, row_count, col_share), half),
            pltpu.VMEM((row_count, col_share), half),
            pltpu.VMEM((row_count, col_share), half),
            pltpu.VMEM((8, TILE, col_share), half),
            pltpu.VMEM((16, TILE, col_share), half),
            pltpu.VMEM((16, TILE, col_share), half),
            pltpu.VMEM((8, TILE, col_share), half),
            pltpu.VMEM((row_count, col_share), single),
            pltpu.VMEM((row_count, 128), single),
            pltpu.VMEM((128, row_count), single),
            pltpu.VMEM((3, row_count, 128), single),
            pltpu.VMEM((3, 8, row_count), single),
            pltpu.VMEM((3, 3, 8, row_count), single),
            dma((4,)),
            dma((4,)),
            dma((4,)),
            dma((4,)),
            dma((2, 4)),
            dma((2, 4)),
            dma((2, 4)),
            dma((2, 4)),
            dma((2,)),
            dma((2,)),
            dma((2,)),
            dma((2,)),
            dma,
            dma((8,)),
            dma((8,)),
            dma((3, 3)),
            dma((3, 3)),
            dma((2, 4)),
            dma((2, 4)),
            dma((4,)),
            dma((4,)),
            pltpu.VMEM((8, row_count, col_share // 2), half),
            pltpu.VMEM((8,) + down_weight.shape[::-1], half),
            pltpu.VMEM((row_count, HID), single),
            pltpu.VMEM((2, 2, row_count, HID), half),
            pltpu.VMEM((2, 2, row_count, HID), half),
            dma((n_hid,)),
            dma((3, n_hid)),
            dma((4, n_hid)),
            dma((4, n_hid)),
            dma((4, n_hid)),
            dma((2, 2)),
            dma((2, 2)),
        ],
        cost_estimate=pl.CostEstimate(
            flops=100_000_000_000, bytes_accessed=400_000_000, transcendentals=0
        ),
        compiler_params=pltpu.CompilerParams(
            collective_id=0, has_side_effects=True, vmem_limit_bytes=60 * 1024 * 1024
        ),
    )(
        key_grads,
        value_grads,
        key_weight,
        value_weight,
        send_index,
        recv_index,
        hidden_mid,
        mlp_out,
        post_gain[None, :],
        final_gain[None, :],
        down_weight.T,
        gate_pre,
        up_pre,
    )


def solution(mesh):
    return jax.shard_map(
        fused_device if mesh.shape["dp"] == 8 and mesh.shape["head"] == 4 else per_device,
        mesh=mesh,
        in_specs=(
            P(None, "dp", "head"),
            P(None, "dp", "head"),
            P(None, "dp", "head"),
            P(None, "dp", "head"),
            P(),
            P("dp", "head"),
            P("dp", "head"),
            P("head"),
            P("head"),
            P("dp", "head"),
            P("dp", "head"),
            P("head", "dp"),
        ),
        out_specs=(P("dp", "head"), P("dp", "head"), P("dp", "head")),
        check_vma=False,
    )
```
